256 devices in a mesh: rep: 16 (over z, x_hi), tp: 16 (over x_lo, y, core).
Axes of the slice: x: 4 (x_hi: 2, x_lo: 2; x = x_hi * 2 + x_lo), y: 4, z: 8, core: 2. Of those that a mesh axis runs over, the one named last changes fastest.
Arguments:
- embeddings: bfloat16 [8, 32, 5120], P(None, 'rep', 'tp'), may hold values from -8 to 8
- w_qkv: bfloat16 [5120, 5120], P('tp'), may hold values from -1 to 1
- q_gain: float32 [128], replicated, may hold values from 0.8 to 3
- w_out: bfloat16 [4096, 5120], P(None, 'tp'), may hold values from -0.09375 to 0.09375
- parent_cache: bfloat16 [16, 16, 8, 1, 2, 128, 512], P('rep', 'tp'), may hold values from -8 to 8
- parent_len: int32 [16, 8], replicated, may hold values from 1 to 16
- route: int32 [16, 16, 2], replicated, may hold values from 0 to 7
- own_pool: bfloat16 [16, 16, 4, 2, 128, 512], P('rep', 'tp'), may hold values from -8 to 8
- own_table: int32 [16, 16, 4], P('rep', 'tp'), may hold values from 0 to 3, each once within a row
- own_len: int32 [16, 2], P('rep'), may hold values from 1 to 4096
Outputs:
- attn_out: bfloat16 [8, 32, 5120], P(None, 'rep', 'tp')
The draws below stay inside these ranges and needn't reach their ends.
Inputs may be any that keep to these rules, and one draw needn't show every extreme that they name: `own_table`: each device's row is a permutation of its 4 pool blocks.
All inputs are finite; a program needn't handle non-finite values.
Results may differ from the reference program's by a relative error of at most 0.0063.
Values may be sent and summed in bfloat16 or wider, within the bound.
No kernel may reach another device: no remote copies, remote signals or barrier semaphores. Data moves between devices by JAX's collectives and lax.ppermute only.
A program may use at most 128 MiB of HBM per device.

```python
import jax
import jax.numpy as jnp
from jax import lax

D = 5120
HEADS = 32
GROUP = 8
HD = 128
BLK = 128
STEPS = 8
RPR = 2
PSEGS = 8
PB = 1
OB = 2
KVH = 4
QD = 4096
KD = 512
ROLLS = 32
N_REP = 16
N_TP = 16


def draw_embeddings(key, part):
    key = jax.random.fold_in(key, 1)
    shape = (STEPS, ROLLS, D)
    base = jax.random.normal(key, shape, jnp.float32)
    return base.astype(jnp.bfloat16)


def draw_w_qkv(key, part):
    key = jax.random.fold_in(key, 2)
    base = jax.random.normal(key, (D, QD + 2 * KD), jnp.float32) * D ** (-0.5)
    return base.astype(jnp.bfloat16)


def draw_q_gain(key, part):
    key = jax.random.fold_in(key, 3)
    return jax.random.uniform(key, (HD,), jnp.float32, 0.8, 1.25)


def draw_parent_cache(key, part):
    key = jax.random.fold_in(key, 4)
    base = jax.random.normal(key, (N_REP, N_TP, PSEGS, PB, 2, BLK, KD), jnp.float32)
    return base.astype(jnp.bfloat16)


def draw_own_pool(key, part):
    key = jax.random.fold_in(key, 5)
    base = jax.random.normal(key, (N_REP, N_TP, RPR * OB, 2, BLK, KD), jnp.float32)
    return base.astype(jnp.bfloat16)


def touch_ends(result, rng, least, top_value):
    longest = result.shape.index(max(result.shape))
    spots = []
    for shift in (0, 1):
        where = [jax.random.randint(jax.random.fold_in(rng, axis), (), 0, length) for axis, length in enumerate(result.shape)]
        where[longest] = (where[longest] + shift) % result.shape[longest]
        spots.append(tuple(where))
    return result.at[spots[0]].set(least).at[spots[1]].set(top_value)


def steps_of(key, extent, cuts, low, high):
    factor_of = 1.0
    for axis_at, shards_of in cuts:
        draws = jax.random.uniform(jax.random.fold_in(jax.random.fold_in(key, 6), axis_at), (shards_of,), jnp.float32, low / len(cuts), high / len(cuts))
        factor_of = factor_of * jnp.repeat(jnp.exp(draws), extent[axis_at] // shards_of).reshape((-1,) + (1,) * (len(extent) - 1 - axis_at))
    return factor_of


def noise(rng, dims, scale, bound, shards=(), kind=jnp.bfloat16):
    level = steps_of(rng, dims, shards, -0.22, 0.18) if shards else 1.0
    values = jax.random.normal(rng, dims, jnp.float32) * scale * level
    return jnp.minimum(jnp.maximum(values, -bound), bound).astype(kind)


def setup_inputs(seed: int = 0) -> dict:
    key_of = jax.random.split(jax.random.key(seed), 11)
    return {
        "embeddings": draw_embeddings(jax.random.fold_in(key_of[10], 71), 0),
        "w_qkv": draw_w_qkv(jax.random.fold_in(key_of[10], 71), 0),
        "q_gain": draw_q_gain(jax.random.fold_in(key_of[10], 71), 0),
        "w_out": noise(key_of[3], (QD, D), QD ** -0.5, 0.09375, ((1, 16),)),
        "parent_cache": draw_parent_cache(jax.random.fold_in(key_of[10], 71), 0),
        "parent_len": touch_ends(jax.random.randint(key_of[5], (N_REP, PSEGS), 1, PB * N_TP + 1), jax.random.fold_in(key_of[5], 1), 1, PB * N_TP).astype(jnp.int32),
        "route": touch_ends(jax.random.randint(key_of[6], (N_REP, N_REP, RPR), 0, PSEGS), jax.random.fold_in(key_of[6], 1), 0, PSEGS - 1).astype(jnp.int32),
        "own_pool": draw_own_pool(jax.random.fold_in(key_of[10], 71), 0),
        "own_table": jax.vmap(lambda own: jax.random.permutation(own, RPR * OB))(jax.random.split(key_of[8], N_REP * N_TP)).reshape((N_REP, N_TP, RPR * OB)).astype(jnp.int32),
        "own_len": touch_ends(jax.random.randint(key_of[9], (N_REP, RPR), 1, OB * N_TP * BLK + 1), jax.random.fold_in(key_of[9], 1), 1, OB * N_TP * BLK).astype(jnp.int32),
    }


norm_eps = 1e-06

def head_norm(values, gain):
    return values * lax.rsqrt(lax.optimization_barrier(jnp.mean(values * values, axis=-1, keepdims=True)) + norm_eps) * gain

def plain_norm(values):
    return values * lax.rsqrt(lax.optimization_barrier(jnp.mean(values * values, axis=-1, keepdims=True)) + norm_eps)

def reference(embeddings, w_qkv, q_gain, w_out, parent_cache, parent_len, route, own_pool, own_table, own_len):
    row_count = STEPS * ROLLS
    projected = jnp.dot(embeddings.reshape(row_count, D), w_qkv, preferred_element_type=jnp.float32)
    queries = head_norm(projected[:, :QD].reshape(row_count, HEADS, HD), q_gain).astype(jnp.bfloat16)
    new_keys = plain_norm(projected[:, QD:QD + KD].reshape(row_count, KVH, HD)).astype(jnp.bfloat16)
    new_values = projected[:, QD + KD:].reshape(row_count, KVH, HD).astype(jnp.bfloat16)
    queries = queries.reshape(STEPS, N_REP, RPR, KVH, GROUP, HD)
    new_keys = new_keys.reshape(STEPS, N_REP, RPR, KVH, HD)
    new_values = new_values.reshape(STEPS, N_REP, RPR, KVH, HD)
    causal = jnp.arange(STEPS)[None, :] <= jnp.arange(STEPS)[:, None]
    piece_span = PB * N_TP * BLK
    parent_span = N_REP * piece_span
    own_span = OB * N_TP * BLK
    owner_index = jnp.arange(N_REP)[:, None]

    def one_replica(replica):
        segments = route[replica]
        pieces = parent_cache[owner_index, :, segments]
        pieces = jnp.transpose(pieces, (1, 0, 3, 2, 4, 5, 6))
        parent_keys = pieces[:, :, :, :, 0].reshape(RPR, parent_span, KVH, HD)
        parent_values = pieces[:, :, :, :, 1].reshape(RPR, parent_span, KVH, HD)
        limits = jnp.transpose(parent_len[owner_index, segments] * BLK, (1, 0))
        parent_ok = (jnp.arange(piece_span)[None, None, :] < limits[:, :, None]).reshape(RPR, parent_span)
        chosen = own_pool[replica][jnp.arange(N_TP)[:, None], own_table[replica]]
        chosen = jnp.transpose(chosen.reshape(N_TP, RPR, OB, 2, BLK, KD), (1, 2, 0, 3, 4, 5))
        own_keys = chosen[:, :, :, 0].reshape(RPR, own_span, KVH, HD)
        own_values = chosen[:, :, :, 1].reshape(RPR, own_span, KVH, HD)
        own_ok = jnp.arange(own_span)[None, :] < own_len[replica][:, None]
        fresh_keys = jnp.transpose(lax.dynamic_index_in_dim(new_keys, replica, 1, keepdims=False), (1, 0, 2, 3))
        fresh_values = jnp.transpose(lax.dynamic_index_in_dim(new_values, replica, 1, keepdims=False), (1, 0, 2, 3))
        asking = jnp.transpose(lax.dynamic_index_in_dim(queries, replica, 1, keepdims=False), (1, 0, 2, 3, 4)).astype(jnp.float32)
        key_rows = jnp.concatenate([parent_keys, own_keys, fresh_keys], axis=1).astype(jnp.float32)
        value_rows = jnp.concatenate([parent_values, own_values, fresh_values], axis=1).astype(jnp.float32)
        cache_ok = jnp.concatenate([parent_ok, own_ok], axis=1)
        cache_len = parent_span + own_span
        allowed = jnp.concatenate([jnp.broadcast_to(cache_ok[:, None, :], (RPR, STEPS, cache_len)), jnp.broadcast_to(causal[None], (RPR, STEPS, STEPS))], axis=2)
        scores = jnp.einsum('jskge,jlke->jskgl', asking, key_rows, precision=lax.Precision.HIGHEST) * HD ** (-0.5)
        scores = jnp.where(allowed[:, :, None, None, :], scores, -jnp.inf)
        highest = lax.optimization_barrier(jnp.max(scores, axis=-1, keepdims=True))
        weights = jnp.exp(scores - highest)
        weight_sum = lax.optimization_barrier(jnp.sum(weights, axis=-1))
        mixed = jnp.einsum('jskgl,jlke->jskge', weights, value_rows, precision=lax.Precision.HIGHEST) / weight_sum[..., None]
        return mixed.reshape(RPR, STEPS, QD)
    attended = lax.map(one_replica, jnp.arange(N_REP))
    attended = jnp.transpose(attended, (2, 0, 1, 3)).reshape(row_count, QD).astype(jnp.bfloat16)
    return jnp.dot(attended, w_out, preferred_element_type=jnp.float32).astype(jnp.bfloat16).reshape(STEPS, ROLLS, D)
```

```python
import functools

import jax
import jax.numpy as jnp
from jax import lax
from jax.experimental import pallas as pl
from jax.experimental.pallas import tpu as pltpu
from jax.sharding import Mesh, PartitionSpec as P

HD = 128
BLK = 128
STEPS = 8
RPR = 2
KVH = 4
PSEGS = 8
N_REP = 16
N_TP = 16
WIDTH = 320
QD = 4096
CHUNK = 40
UNROLL = 2

EPS = 1e-06
FAR = -1e30
SCALE2 = HD ** (-0.5) * 1.4426950408889634
MIB = 1024 * 1024

TP = ("xl", "y", "c")
XC = ("xl", "c")
REP = ("z", "xh")

VMEM = pltpu.VMEM
SMEM = pltpu.SMEM


def nt(a, b):
    return lax.dot_general(a, b, (((1,), (1,)), ((), ())), preferred_element_type=jnp.float32)


def start_kernel(emb, w, parent, own, table, sums, *rest):
    outs, (wide, wsem, sem) = rest[:8], rest[8:]
    xl = lax.axis_index("xl")
    c = lax.axis_index("c")
    moves = []
    for d in (2, 3, 1, 0):
        head = (xl ^ (d // 2)) * 2 + (c ^ (d % 2))
        lanes = pl.ds(pl.multiple_of(head * HD, HD), HD)
        moves.append(pltpu.make_async_copy(parent.at[:, :, :, lanes], outs[d], sem.at[d, 0]))
        for e in range(4):
            moves.append(
                pltpu.make_async_copy(
                    own.at[table[0, 0, e], :, :, lanes], outs[4 + d].at[e], sem.at[d, 1 + e]
                )
            )
    loads = [
        pltpu.make_async_copy(
            w.at[:, pl.ds(n * 1024, 1024)], wide.at[:, pl.ds(n * 1024, 1024)], wsem.at[n]
        )
        for n in range(5)
    ]
    for copy in moves[:10] + loads + moves[10:]:
        copy.start()
    rows = [emb[s].astype(jnp.float32) for s in range(STEPS)]
    flat = jnp.concatenate([rows[s][j : j + 1] for j in range(RPR) for s in range(STEPS)], axis=0)
    flat = flat.astype(jnp.bfloat16)
    for n in range(5):
        loads[n].wait()
        part = jnp.dot(
            flat, wide[:, n * 1024 : n * 1024 + 1024], preferred_element_type=jnp.float32
        )
        for k in range(KVH):
            for y in range(4):
                t = (k // 2) * 8 + y * 2 + k % 2
                if n == k:
                    for j in range(RPR):
                        for g in range(2):
                            col = (2 * y + g) * HD
                            sums[t, j * 16 + g * 8 : j * 16 + g * 8 + 8, :] = part[
                                j * 8 : j * 8 + 8, col : col + HD
                            ]
                elif n == 4:
                    col = (y // 2) * 512 + k * HD
                    sums[t, 32:40, :] = part[(y % 2) * 8 : (y % 2) * 8 + 8, col : col + HD]
    for copy in moves:
        copy.wait()


def start(emb, w_qkv, parent, own, table):
    piece = jax.ShapeDtypeStruct((PSEGS, 2, BLK, HD), jnp.bfloat16)
    small = jax.ShapeDtypeStruct((4, 2, BLK, HD), jnp.bfloat16)
    return pl.pallas_call(
        start_kernel,
        in_specs=[
            pl.BlockSpec(memory_space=VMEM),
            pl.BlockSpec(memory_space=pltpu.HBM),
            pl.BlockSpec(memory_space=pltpu.HBM),
            pl.BlockSpec(memory_space=pltpu.HBM),
            pl.BlockSpec(memory_space=SMEM),
        ],
        out_specs=[pl.BlockSpec(memory_space=VMEM)] * 9,
        out_shape=[jax.ShapeDtypeStruct((N_TP, CHUNK, HD), jnp.float32)] + [piece] * 4 + [small] * 4,
        scratch_shapes=[
            VMEM((WIDTH, 5120), jnp.bfloat16),
            pltpu.SemaphoreType.DMA((5,)),
            pltpu.SemaphoreType.DMA((4, 5)),
        ],
        compiler_params=pltpu.CompilerParams(vmem_limit_bytes=16 * MIB),
        cost_estimate=pl.CostEstimate(flops=2 * 16 * WIDTH * 5120, bytes_accessed=9600000, transcendentals=0),
        name="start",
    )(emb, w_qkv, parent, own, table)


def norm_kernel(parts, gain, out):
    y = lax.axis_index("y")
    total = parts[0]
    for t in range(1, N_TP):
        total = total + parts[t]
    normed = total * lax.rsqrt(jnp.mean(total * total, axis=-1, keepdims=True) + EPS)
    row = lax.broadcasted_iota(jnp.int32, (CHUNK, HD), 0)
    tail = jnp.where(jnp.broadcast_to(y, (CHUNK, HD)) < 2, normed, total)
    result = jnp.where(row < 32, normed * gain[...], tail).astype(jnp.bfloat16)
    for r in range(N_REP):
        out[r] = result


def norm_heads(parts, gain):
    return pl.pallas_call(
        norm_kernel,
        in_specs=[pl.BlockSpec(memory_space=VMEM)] * 2,
        out_specs=pl.BlockSpec(memory_space=VMEM),
        out_shape=jax.ShapeDtypeStruct((N_REP, CHUNK, HD), jnp.bfloat16),
        compiler_params=pltpu.CompilerParams(vmem_limit_bytes=16 * MIB),
        cost_estimate=pl.CostEstimate(flops=400000, bytes_accessed=1000000, transcendentals=64),
        name="norm_heads",
    )(parts, gain)


def soft(scores):
    top = jnp.max(scores, axis=0, keepdims=True)
    weights = jnp.exp2(scores - top)
    return top, jnp.sum(weights, axis=0, keepdims=True), weights.astype(jnp.bfloat16)


def stat_rows(level):
    high = level.astype(jnp.bfloat16).astype(jnp.float32)
    rest = level - high
    middle = rest.astype(jnp.bfloat16).astype(jnp.float32)
    row = lax.broadcasted_iota(jnp.int32, (8, HD), 0)
    return jnp.where(
        row == 0, high, jnp.where(row == 1, middle, jnp.where(row == 2, rest - middle, 0.0))
    )


def attend_kernel(segs, plen, olen, *refs):
    qin, kvs, own, outs = refs[0:4], refs[4:8], refs[8:12], refs[12:16]
    vt, qs, save, mix = refs[16:20]
    xl = lax.axis_index("xl")
    y = lax.axis_index("y")
    c = lax.axis_index("c")
    me = lax.axis_index("z") * 2 + lax.axis_index("xh")
    owners = [(xl ^ (d // 2)) * 8 + y * 2 + (c ^ (d % 2)) for d in range(4)]
    lane = lax.broadcasted_iota(jnp.int32, (1, HD), 1)
    left = lane < 64
    for n in range(4):
        qs[(y - n + 4) % 4] = qin[n][...]

    for d in range(4):
        for i in range(PSEGS):
            vt[d, i] = kvs[d][i, 1].T
        for i in range(4):
            vt[d, PSEGS + i] = own[d][i, 1].T

    def queries_of(r):
        zero = jnp.zeros((64, HD), jnp.bfloat16)
        q0 = jnp.concatenate([qs[p, r, 0:16, :] for p in range(4)], axis=0)
        q1 = jnp.concatenate([qs[p, r, 16:32, :] for p in range(4)], axis=0)
        return jnp.concatenate(
            [jnp.concatenate([q0, zero], axis=1), jnp.concatenate([zero, q1], axis=1)], axis=0
        )

    def emit(r, slot, top, total, mixed):
        mix[slot] = mixed * (1.0 / total)
        tail = stat_rows(top + jnp.log2(total))
        for n in range(4):
            part = mix[slot, pl.ds(pl.multiple_of(((y + n) % 4) * 32, 32), 32), :]
            outs[n][r] = jnp.concatenate([part, tail], axis=0).astype(jnp.bfloat16)

    def one(r, slot):
        s0 = segs[r, 0]
        s1 = segs[r, 1]
        keys = jnp.concatenate(
            [jnp.concatenate([kvs[d][s0, 0], kvs[d][s1, 0]], axis=1) for d in range(4)], axis=0
        )
        scores = nt(keys, queries_of(r)) * SCALE2
        limit = jnp.where(left, plen[0, s0], plen[0, s1])
        scores = jnp.concatenate(
            [
                scores[d * BLK : d * BLK + BLK] + jnp.where(limit > owners[d], 0.0, FAR)
                for d in range(4)
            ],
            axis=0,
        )
        top, total, weights = soft(scores)
        values = jnp.concatenate(
            [jnp.concatenate([vt[d, s] for d in range(4)], axis=1) for s in (s0, s1)], axis=0
        )
        both = jnp.dot(values, weights, preferred_element_type=jnp.float32)
        mixed = jnp.where(left, both[0:HD], both[HD : 2 * HD])
        emit(r, slot, top, total, mixed)
        save[r, 0:HD] = mixed
        save[r, HD : HD + 1] = top
        save[r, HD + 1 : HD + 2] = total

    def several(i, carry):
        for n in range(UNROLL):
            one(i * UNROLL + n, n)
        return carry

    lax.fori_loop(0, N_REP // UNROLL, several, 0)

    fresh_k = [qs[j, me, 32:40, :].astype(jnp.float32) for j in range(2)]
    fresh_v = [qs[2 + j, me, 32:40, :].astype(jnp.float32) for j in range(2)]
    pad = jnp.zeros((BLK - 8, HD), jnp.float32)
    fresh_k = [jnp.concatenate([a, pad], axis=0).astype(jnp.bfloat16) for a in fresh_k]
    fresh_v = [jnp.concatenate([a, pad], axis=0).T.astype(jnp.bfloat16) for a in fresh_v]
    blocks = [(d, b) for d in range(4) for b in range(2)]
    keys = jnp.concatenate(
        [jnp.concatenate([own[d][b, 0], own[d][2 + b, 0]], axis=1) for d, b in blocks]
        + [jnp.concatenate(fresh_k, axis=1)],
        axis=0,
    )
    scores = nt(keys, queries_of(me)) * SCALE2
    limit = jnp.where(left, olen[0, 0], olen[0, 1])
    token = lax.broadcasted_iota(jnp.int32, (BLK, HD), 0)
    step = lax.broadcasted_iota(jnp.int32, (BLK, HD), 1) % 8
    parts = []
    for n, (d, b) in enumerate(blocks):
        position = token + (b * N_TP + owners[d]) * BLK
        parts.append(jnp.where(position < limit, scores[n * BLK : n * BLK + BLK], FAR))
    here = jnp.broadcast_to(y, (BLK, HD)) == 0
    parts.append(jnp.where((token <= step) & here, scores[8 * BLK : 9 * BLK], FAR))
    top, total, weights = soft(jnp.concatenate(parts, axis=0))
    values = jnp.concatenate(
        [
            jnp.concatenate([vt[d, 8 + 2 * j + b] for d, b in blocks] + [fresh_v[j]], axis=1)
            for j in range(2)
        ],
        axis=0,
    )
    both = jnp.dot(values, weights, preferred_element_type=jnp.float32)
    mixed = jnp.where(left, both[0:HD], both[HD : 2 * HD])
    top_a = save[me, HD : HD + 1]
    peak = jnp.maximum(top_a, top)
    scale_a = jnp.exp2(top_a - peak)
    scale_b = jnp.exp2(top - peak)
    emit(
        me,
        0,
        peak,
        save[me, HD + 1 : HD + 2] * scale_a + total * scale_b,
        save[me, 0:HD] * scale_a + mixed * scale_b,
    )


def attend(segs, plen, olen, queries, kvs, own):
    chunk = jax.ShapeDtypeStruct((N_REP, CHUNK, HD), jnp.bfloat16)
    return pl.pallas_call(
        attend_kernel,
        in_specs=[pl.BlockSpec(memory_space=SMEM)] * 3 + [pl.BlockSpec(memory_space=VMEM)] * 12,
        out_specs=[pl.BlockSpec(memory_space=VMEM)] * 4,
        out_shape=[chunk] * 4,
        scratch_shapes=[
            VMEM((4, 12, HD, BLK), jnp.bfloat16),
            VMEM((4, N_REP, CHUNK, HD), jnp.bfloat16),
            VMEM((N_REP, HD + 8, HD), jnp.float32),
            VMEM((UNROLL, HD, HD), jnp.float32),
        ],
        compiler_params=pltpu.CompilerParams(vmem_limit_bytes=24 * MIB),
        cost_estimate=pl.CostEstimate(flops=1600000000, bytes_accessed=4500000, transcendentals=1200000),
        name="attend",
    )(segs, plen, olen, *queries, *kvs, *own)


def level_of(part):
    return jnp.sum(part[32:40].astype(jnp.float32), axis=0, keepdims=True)


def fold_kernel(p0, p1, p2, p3, out):
    def one(r, carry):
        parts = [p[r] for p in (p0, p1, p2, p3)]
        levels = [level_of(part) for part in parts]
        top = jnp.maximum(
            jnp.maximum(levels[0], levels[1]), jnp.maximum(levels[2], levels[3])
        )
        weights = [jnp.exp2(level - top) for level in levels]
        total = (weights[0] + weights[1]) + (weights[2] + weights[3])
        share = 1.0 / total
        mixed = jnp.zeros((32, HD), jnp.float32)
        for part, weight in zip(parts, weights):
            mixed = mixed + part[0:32].astype(jnp.float32) * (weight * share)
        out[r] = jnp.concatenate([mixed, stat_rows(top + jnp.log2(total))], axis=0).astype(
            jnp.bfloat16
        )
        return carry

    lax.fori_loop(0, N_REP, one, 0, unroll=4)


def fold(parts):
    return pl.pallas_call(
        fold_kernel,
        in_specs=[pl.BlockSpec(memory_space=VMEM)] * 4,
        out_specs=pl.BlockSpec(memory_space=VMEM),
        out_shape=jax.ShapeDtypeStruct((N_REP, CHUNK, HD), jnp.bfloat16),
        compiler_params=pltpu.CompilerParams(vmem_limit_bytes=16 * MIB),
        cost_estimate=pl.CostEstimate(flops=1000000, bytes_accessed=800000, transcendentals=8192),
        name="fold_blocks",
    )(*parts)


def merge_kernel(parts, out):
    level = jnp.concatenate([level_of(parts[i]) for i in range(N_REP)], axis=0)
    weight = jnp.exp2(level - jnp.max(level, axis=0, keepdims=True))
    weight = weight * (1.0 / jnp.sum(weight, axis=0, keepdims=True))
    total = jnp.zeros((32, HD), jnp.float32)
    for i in range(N_REP):
        total = total + parts[i, 0:32, :].astype(jnp.float32) * weight[i : i + 1]
    result = total.astype(jnp.bfloat16)
    for t in range(N_TP):
        out[t] = result


def merge(parts):
    return pl.pallas_call(
        merge_kernel,
        in_specs=[pl.BlockSpec(memory_space=VMEM)],
        out_specs=pl.BlockSpec(memory_space=VMEM),
        out_shape=jax.ShapeDtypeStruct((N_TP, 32, HD), jnp.bfloat16),
        compiler_params=pltpu.CompilerParams(vmem_limit_bytes=16 * MIB),
        cost_estimate=pl.CostEstimate(flops=200000, bytes_accessed=300000, transcendentals=2048),
        name="merge_owners",
    )(parts)


def final_kernel(attended, w_out, out, rows):
    for k in range(KVH):
        base = (k // 2) * 8 + k % 2
        tile = jnp.concatenate(
            [attended[base + 2 * p].astype(jnp.float32) for p in range(4)], axis=0
        )
        turned = tile.T
        for j in range(RPR):
            for g in range(8):
                rows[k * 8 + g, pl.ds(j, 8, stride=2), :] = turned[
                    j * 64 + g * 8 : j * 64 + g * 8 + 8
                ]
    wide = jnp.concatenate([rows[h].astype(jnp.bfloat16) for h in range(QD // HD)], axis=1)
    result = nt(wide, w_out[...])
    for s in range(STEPS):
        out[s] = result[2 * s : 2 * s + 2].astype(jnp.bfloat16)


def final(attended, w_out):
    return pl.pallas_call(
        final_kernel,
        in_specs=[pl.BlockSpec(memory_space=VMEM)] * 2,
        out_specs=pl.BlockSpec(memory_space=VMEM),
        out_shape=jax.ShapeDtypeStruct((STEPS, RPR, WIDTH), jnp.bfloat16),
        scratch_shapes=[VMEM((QD // HD, 16, HD), jnp.float32)],
        compiler_params=pltpu.CompilerParams(vmem_limit_bytes=16 * MIB),
        cost_estimate=pl.CostEstimate(flops=2 * 16 * QD * WIDTH, bytes_accessed=2900000, transcendentals=0),
        name="final",
    )(attended, w_out.T)


def swap(x, axes):
    return lax.all_to_all(x, axes, 0, 0, tiled=True)


def body(
    embeddings, w_qkv, q_gain, w_out, parent_cache, parent_len, route, own_pool, own_table, own_len
):
    me = lax.axis_index(REP)
    parent = parent_cache.reshape(PSEGS, 2, BLK, KVH * HD)
    own = own_pool.reshape(4, 2, BLK, KVH * HD)
    sums, *cut = start(embeddings, w_qkv, parent, own, own_table)

    def shift(x, d):
        return lax.ppermute(x, XC, [(i, i ^ d) for i in range(4)]) if d else x

    def along(x, n):
        return lax.ppermute(x, "y", [(i, (i + n) % 4) for i in range(4)]) if n else x

    kv2 = shift(cut[2], 2)
    parts = swap(sums, TP)
    heads = norm_heads(parts, q_gain.reshape(1, HD))
    heads, kv2, cut = lax.optimization_barrier((heads, kv2, cut))
    kv3 = shift(cut[3], 3)
    gathered = swap(heads, REP)
    gathered, kv3, cut = lax.optimization_barrier((gathered, kv3, cut))
    kvs = [cut[0], shift(cut[1], 1), kv2, kv3]
    owns = [shift(cut[4 + d], d) for d in range(4)]
    queries = [along(gathered, n) for n in range(4)]
    segs = lax.dynamic_index_in_dim(route, me, 1, keepdims=False)
    plen = lax.dynamic_index_in_dim(parent_len, me, 0, keepdims=True)
    partial = attend(segs, plen, own_len, queries, kvs, owns)
    folded = fold([along(partial[n], n) for n in range(4)])
    attended = merge(swap(folded, REP))
    everyone = swap(attended, TP)
    return final(everyone, w_out)


def solution(mesh):
    fine = Mesh(mesh.devices.reshape(8, 2, 2, 4, 2), ("z", "xh", "xl", "y", "c"))
    in_specs = (
        P(None, REP, TP),
        P(TP, None),
        P(),
        P(None, TP),
        P(REP, TP, None, None, None, None, None),
        P(),
        P(),
        P(REP, TP, None, None, None, None),
        P(REP, TP, None),
        P(REP, None),
    )
    out_specs = P(None, REP, TP)
    return jax.shard_map(body, mesh=fine, in_specs=in_specs, out_specs=out_specs, check_vma=False)
```

```python
import functools

import jax
import jax.numpy as jnp
from jax import lax
from jax.experimental import pallas as pl
from jax.experimental.pallas import tpu as pltpu
from jax.sharding import Mesh, PartitionSpec as P

HD = 128
BLK = 128
STEPS = 8
RPR = 2
KVH = 4
PSEGS = 8
N_REP = 16
N_TP = 16
WIDTH = 320
QD = 4096
CHUNK = 40
UNROLL = 4
START_MIB = 16

EPS = 1e-06
FAR = -1e30
SCALE2 = HD ** (-0.5) * 1.4426950408889634
MIB = 1024 * 1024

TP = ("xl", "y", "c")
REP = ("z", "xh")

VMEM = pltpu.VMEM
SMEM = pltpu.SMEM


def nt(a, b):
    return lax.dot_general(a, b, (((1,), (1,)), ((), ())), preferred_element_type=jnp.float32)


def lanes_of(head):
    return pl.ds(pl.multiple_of(head * HD, HD), HD)


def half_of(xl, y):
    return xl ^ (y % 2)


def start_kernel(emb_hbm, w, parent, own, table_hbm, sums, *rest):
    outs, (wide, emb, table, wsem, sem) = rest[0:5], rest[5:]
    c = lax.axis_index("c")
    h2 = half_of(lax.axis_index("xl"), lax.axis_index("y"))
    first = [
        pltpu.make_async_copy(table_hbm.at[0], table, wsem.at[5]),
        pltpu.make_async_copy(emb_hbm, emb, wsem.at[6]),
    ]
    loads = [
        pltpu.make_async_copy(
            w.at[:, pl.ds(n * 1024, 1024)], wide.at[:, pl.ds(n * 1024, 1024)], wsem.at[n]
        )
        for n in range(5)
    ]
    plans = [(2, 0, 4), (2, 4, 4), (3, 0, 4), (3, 4, 4), (1, 0, 8)]
    moves = []
    for n, (d, low, count) in enumerate(plans):
        lanes = lanes_of((h2 ^ (d // 2)) * 2 + (c ^ (d % 2)))
        moves.append(
            [
                pltpu.make_async_copy(
                    parent.at[pl.ds(low, count), :, :, lanes],
                    outs[n].at[pl.ds(0, count)],
                    sem.at[n, 0],
                )
            ]
        )
    for copy in first + moves[0] + moves[1] + loads + moves[2] + moves[3] + moves[4]:
        copy.start()
    first[0].wait()
    for n, (d, low, count) in enumerate(plans):
        lanes = lanes_of((h2 ^ (d // 2)) * 2 + (c ^ (d % 2)))
        for i in range(count // 2):
            moves[n].append(
                pltpu.make_async_copy(
                    own.at[table[0, low // 2 + i], :, :, lanes],
                    outs[n].at[count + i],
                    sem.at[n, 1 + i],
                )
            )
            moves[n][-1].start()
    first[1].wait()
    rows = [emb[s].astype(jnp.float32) for s in range(STEPS)]
    flat = jnp.concatenate([rows[s][j : j + 1] for j in range(RPR) for s in range(STEPS)], axis=0)
    flat = flat.astype(jnp.bfloat16)
    for n in range(5):
        loads[n].wait()
        part = jnp.dot(
            flat, wide[:, n * 1024 : n * 1024 + 1024], preferred_element_type=jnp.float32
        )
        for k in range(KVH):
            for y in range(4):
                t = half_of(k // 2, y) * 8 + y * 2 + k % 2
                if n == k:
                    for j in range(RPR):
                        for g in range(2):
                            col = (2 * y + g) * HD
                            sums[t, j * 16 + g * 8 : j * 16 + g * 8 + 8, :] = part[
                                j * 8 : j * 8 + 8, col : col + HD
                            ]
                elif n == 4:
                    col = (y // 2) * 512 + k * HD
                    sums[t, 32:40, :] = part[(y % 2) * 8 : (y % 2) * 8 + 8, col : col + HD]
    for group in moves:
        for copy in group:
            copy.wait()


def start(emb, w_qkv, parent, own, table):
    shapes = [(6, 2, BLK, HD)] * 4 + [(12, 2, BLK, HD)]
    return pl.pallas_call(
        start_kernel,
        in_specs=[pl.BlockSpec(memory_space=pltpu.HBM)] * 5,
        out_specs=[pl.BlockSpec(memory_space=VMEM)] * 6,
        out_shape=[jax.ShapeDtypeStruct((N_TP, CHUNK, HD), jnp.float32)]
        + [jax.ShapeDtypeStruct(shape, jnp.bfloat16) for shape in shapes],
        scratch_shapes=[
            VMEM((WIDTH, 5120), jnp.bfloat16),
            VMEM((STEPS, RPR, WIDTH), jnp.bfloat16),
            SMEM((1, 4), jnp.int32),
            pltpu.SemaphoreType.DMA((7,)),
            pltpu.SemaphoreType.DMA((5, 5)),
        ],
        compiler_params=pltpu.CompilerParams(vmem_limit_bytes=START_MIB * MIB),
        cost_estimate=pl.CostEstimate(flops=2 * 16 * WIDTH * 5120, bytes_accessed=9000000, transcendentals=0),
        name="start",
    )(*[pltpu.with_memory_space_constraint(a, pltpu.HBM) for a in (emb, w_qkv, parent, own, table)])


def norm_kernel(parts, gain, out):
    y = lax.axis_index("y")
    total = parts[0]
    for t in range(1, N_TP):
        total = total + parts[t]
    normed = total * lax.rsqrt(jnp.mean(total * total, axis=-1, keepdims=True) + EPS)
    row = lax.broadcasted_iota(jnp.int32, (CHUNK, HD), 0)
    tail = jnp.where(jnp.broadcast_to(y, (CHUNK, HD)) < 2, normed, total)
    result = jnp.where(row < 32, normed * gain[...], tail).astype(jnp.bfloat16)
    for r in range(N_REP):
        out[r] = result


def norm_heads(parts, gain):
    return pl.pallas_call(
        norm_kernel,
        in_specs=[pl.BlockSpec(memory_space=VMEM)] * 2,
        out_specs=pl.BlockSpec(memory_space=VMEM),
        out_shape=jax.ShapeDtypeStruct((N_REP, CHUNK, HD), jnp.bfloat16),
        compiler_params=pltpu.CompilerParams(vmem_limit_bytes=16 * MIB),
        cost_estimate=pl.CostEstimate(flops=400000, bytes_accessed=600000, transcendentals=64),
        name="norm_heads",
    )(parts, gain)


def soft(scores):
    top = jnp.max(scores, axis=0, keepdims=True)
    weights = jnp.exp2(scores - top)
    return top, jnp.sum(weights, axis=0, keepdims=True), weights.astype(jnp.bfloat16)


def stat_rows(level):
    high = level.astype(jnp.bfloat16).astype(jnp.float32)
    rest = level - high
    middle = rest.astype(jnp.bfloat16).astype(jnp.float32)
    row = lax.broadcasted_iota(jnp.int32, (8, HD), 0)
    return jnp.where(
        row == 0, high, jnp.where(row == 1, middle, jnp.where(row == 2, rest - middle, 0.0))
    )


def pair_queries(parts):
    zero = jnp.zeros((64, HD), jnp.bfloat16)
    q0 = jnp.concatenate([part[0:16] for part in parts], axis=0)
    q1 = jnp.concatenate([part[16:32] for part in parts], axis=0)
    return jnp.concatenate(
        [jnp.concatenate([q0, zero], axis=1), jnp.concatenate([zero, q1], axis=1)], axis=0
    )


def attend_kernel(segs, plen, olen, table, parent, own, *refs):
    qin, (kv1, a2, b2, a3, b3), outs = refs[0:4], refs[4:9], refs[9:13]
    ks, vt, qs, save, near, sem = refs[13:19]
    xl = lax.axis_index("xl")
    y = lax.axis_index("y")
    c = lax.axis_index("c")
    me = lax.axis_index("z") * 2 + lax.axis_index("xh")
    lanes = lanes_of(half_of(xl, y) * 2 + c)
    loads = [
        pltpu.make_async_copy(
            parent.at[:, :, :, lanes], near.at[pl.ds(0, PSEGS)], sem.at[0]
        )
    ] + [
        pltpu.make_async_copy(
            own.at[table[0, 0, e], :, :, lanes], near.at[PSEGS + e], sem.at[1 + e]
        )
        for e in range(4)
    ]
    for copy in loads:
        copy.start()
    owners = [(xl ^ (d // 2)) * 8 + y * 2 + (c ^ (d % 2)) for d in range(4)]
    owners_b = [xl * 8 + (y ^ (d // 2)) * 2 + (c ^ (d % 2)) for d in range(4)]
    left = lax.broadcasted_iota(jnp.int32, (1, HD), 1) < 64
    for n in range(4):
        qs[(y - n + 4) % 4] = qin[n][...]
    for d, first, second in ((1, kv1, None), (2, a2, b2), (3, a3, b3), (0, near, None)):
        if d == 0:
            for copy in loads:
                copy.wait()
        for i in range(12):
            if second is None:
                piece, at = first, i
            elif i < PSEGS:
                piece, at = (first, i) if i < 4 else (second, i - 4)
            else:
                piece, at = (first, i - 4) if i < 10 else (second, i - 6)
            ks[d, i] = piece[at, 0]
            vt[d, i] = piece[at, 1].T

    def emit(r, mixed, level):
        save[r, 0:HD] = mixed
        save[r, HD : HD + 1] = level
        tail = stat_rows(level)
        for n in range(4):
            part = save[r, pl.ds(pl.multiple_of(((y + n) % 4) * 32, 32), 32), :]
            outs[n][r] = jnp.concatenate([part, tail], axis=0).astype(jnp.bfloat16)

    def one(r):
        s0 = segs[r, 0]
        s1 = segs[r, 1]
        keys = jnp.concatenate(
            [jnp.concatenate([ks[d, s0], ks[d, s1]], axis=1) for d in range(4)], axis=0
        )
        scores = nt(keys, pair_queries([qs[p, r] for p in range(4)])) * SCALE2
        limit = jnp.where(left, plen[0, s0], plen[0, s1])
        masked = []
        for d in range(4):
            owner = jnp.where(
                left,
                jnp.where(s0 < 4, owners[d], owners_b[d]),
                jnp.where(s1 < 4, owners[d], owners_b[d]),
            )
            masked.append(scores[d * BLK : d * BLK + BLK] + jnp.where(limit > owner, 0.0, FAR))
        top, total, weights = soft(jnp.concatenate(masked, axis=0))
        values = jnp.concatenate(
            [jnp.concatenate([vt[d, s] for d in range(4)], axis=1) for s in (s0, s1)], axis=0
        )
        both = jnp.dot(values, weights, preferred_element_type=jnp.float32)
        mixed = jnp.where(left, both[0:HD], both[HD : 2 * HD]) * (1.0 / total)
        emit(r, mixed, top + jnp.log2(total))

    def several(i, carry):
        for n in range(UNROLL):
            one(i * UNROLL + n)
        return carry

    lax.fori_loop(0, N_REP // UNROLL, several, 0)

    pad = jnp.zeros((BLK - 8, HD), jnp.float32)
    fresh = [qs[p, me][32:40].astype(jnp.float32) for p in range(4)]
    fresh = [jnp.concatenate([part, pad], axis=0) for part in fresh]
    blocks = [(d, b) for d in range(4) for b in range(2)]
    keys = [jnp.concatenate([ks[d, 8 + b], ks[d, 10 + b]], axis=1) for d, b in blocks]
    keys.append(jnp.concatenate(fresh[0:2], axis=1).astype(jnp.bfloat16))
    scores = nt(jnp.concatenate(keys, axis=0), pair_queries([qs[p, me] for p in range(4)])) * SCALE2
    limit = jnp.where(left, olen[0, 0], olen[0, 1])
    token = lax.broadcasted_iota(jnp.int32, (BLK, HD), 0)
    step = lax.broadcasted_iota(jnp.int32, (BLK, HD), 1) % 8
    masked = []
    for n, (d, b) in enumerate(blocks):
        owner = jnp.where(left, owners[d], owners_b[d])
        position = token + (b * N_TP + owner) * BLK
        masked.append(jnp.where(position < limit, scores[n * BLK : n * BLK + BLK], FAR))
    here = jnp.broadcast_to(y, (BLK, HD)) == 0
    masked.append(jnp.where((token <= step) & here, scores[8 * BLK : 9 * BLK], FAR))
    top, total, weights = soft(jnp.concatenate(masked, axis=0))
    values = jnp.concatenate(
        [
            jnp.concatenate(
                [vt[d, 8 + 2 * j + b] for d, b in blocks] + [fresh[2 + j].T.astype(jnp.bfloat16)],
                axis=1,
            )
            for j in range(2)
        ],
        axis=0,
    )
    both = jnp.dot(values, weights, preferred_element_type=jnp.float32)
    mixed = jnp.where(left, both[0:HD], both[HD : 2 * HD]) * (1.0 / total)
    level = top + jnp.log2(total)
    before = save[me, HD : HD + 1]
    peak = jnp.maximum(before, level)
    scale_a = jnp.exp2(before - peak)
    scale_b = jnp.exp2(level - peak)
    total = scale_a + scale_b
    mixed = save[me, 0:HD] * (scale_a / total) + mixed * (scale_b / total)
    emit(me, mixed, peak + jnp.log2(total))


def attend(segs, plen, olen, table, parent, own, queries, pieces):
    chunk = jax.ShapeDtypeStruct((N_REP, CHUNK, HD), jnp.bfloat16)
    return pl.pallas_call(
        attend_kernel,
        in_specs=[pl.BlockSpec(memory_space=SMEM)] * 4
        + [pl.BlockSpec(memory_space=pltpu.HBM)] * 2
        + [pl.BlockSpec(memory_space=VMEM)] * 9,
        out_specs=[pl.BlockSpec(memory_space=VMEM)] * 4,
        out_shape=[chunk] * 4,
        scratch_shapes=[
            VMEM((4, 12, BLK, HD), jnp.bfloat16),
            VMEM((4, 12, HD, BLK), jnp.bfloat16),
            VMEM((4, N_REP, CHUNK, HD), jnp.bfloat16),
            VMEM((N_REP, HD + 8, HD), jnp.float32),
            VMEM((12, 2, BLK, HD), jnp.bfloat16),
            pltpu.SemaphoreType.DMA((5,)),
        ],
        compiler_params=pltpu.CompilerParams(vmem_limit_bytes=24 * MIB),
        cost_estimate=pl.CostEstimate(flops=1600000000, bytes_accessed=4500000, transcendentals=1200000),
        name="attend",
    )(
        segs,
        plen,
        olen,
        table,
        pltpu.with_memory_space_constraint(parent, pltpu.HBM),
        pltpu.with_memory_space_constraint(own, pltpu.HBM),
        *queries,
        *pieces,
    )


def level_of(part):
    return jnp.sum(part[32:40].astype(jnp.float32), axis=0, keepdims=True)


def fold_kernel(p0, p1, p2, p3, out):
    def one(r, carry):
        parts = [p[r] for p in (p0, p1, p2, p3)]
        levels = [level_of(part) for part in parts]
        top = jnp.maximum(
            jnp.maximum(levels[0], levels[1]), jnp.maximum(levels[2], levels[3])
        )
        weights = [jnp.exp2(level - top) for level in levels]
        total = (weights[0] + weights[1]) + (weights[2] + weights[3])
        share = 1.0 / total
        mixed = jnp.zeros((32, HD), jnp.float32)
        for part, weight in zip(parts, weights):
            mixed = mixed + part[0:32].astype(jnp.float32) * (weight * share)
        out[r] = jnp.concatenate([mixed, stat_rows(top + jnp.log2(total))], axis=0).astype(
            jnp.bfloat16
        )
        return carry

    lax.fori_loop(0, N_REP, one, 0, unroll=4)


def fold(parts):
    return pl.pallas_call(
        fold_kernel,
        in_specs=[pl.BlockSpec(memory_space=VMEM)] * 4,
        out_specs=pl.BlockSpec(memory_space=VMEM),
        out_shape=jax.ShapeDtypeStruct((N_REP, CHUNK, HD), jnp.bfloat16),
        compiler_params=pltpu.CompilerParams(vmem_limit_bytes=16 * MIB),
        cost_estimate=pl.CostEstimate(flops=1000000, bytes_accessed=800000, transcendentals=8192),
        name="fold_blocks",
    )(*parts)


def merge_kernel(parts, out):
    level = jnp.concatenate([level_of(parts[i]) for i in range(N_REP)], axis=0)
    weight = jnp.exp2(level - jnp.max(level, axis=0, keepdims=True))
    weight = weight * (1.0 / jnp.sum(weight, axis=0, keepdims=True))
    total = jnp.zeros((32, HD), jnp.float32)
    for i in range(N_REP):
        total = total + parts[i, 0:32, :].astype(jnp.float32) * weight[i : i + 1]
    result = total.astype(jnp.bfloat16)
    for t in range(N_TP):
        out[t] = result


def merge(parts):
    return pl.pallas_call(
        merge_kernel,
        in_specs=[pl.BlockSpec(memory_space=VMEM)],
        out_specs=pl.BlockSpec(memory_space=VMEM),
        out_shape=jax.ShapeDtypeStruct((N_TP, 32, HD), jnp.bfloat16),
        compiler_params=pltpu.CompilerParams(vmem_limit_bytes=16 * MIB),
        cost_estimate=pl.CostEstimate(flops=200000, bytes_accessed=300000, transcendentals=2048),
        name="merge_owners",
    )(parts)


def final_kernel(attended, w_out, out, rows):
    for k in range(KVH):
        tile = jnp.concatenate(
            [
                attended[half_of(k // 2, p) * 8 + p * 2 + k % 2].astype(jnp.float32)
                for p in range(4)
            ],
            axis=0,
        )
        turned = tile.T
        for j in range(RPR):
            for g in range(8):
                rows[k * 8 + g, pl.ds(j, 8, stride=2), :] = turned[
                    j * 64 + g * 8 : j * 64 + g * 8 + 8
                ]
    wide = jnp.concatenate([rows[h].astype(jnp.bfloat16) for h in range(QD // HD)], axis=1)
    result = nt(wide, w_out[...])
    for s in range(STEPS):
        out[s] = result[2 * s : 2 * s + 2].astype(jnp.bfloat16)


def final(attended, w_out):
    return pl.pallas_call(
        final_kernel,
        in_specs=[pl.BlockSpec(memory_space=VMEM)] * 2,
        out_specs=pl.BlockSpec(memory_space=VMEM),
        out_shape=jax.ShapeDtypeStruct((STEPS, RPR, WIDTH), jnp.bfloat16),
        scratch_shapes=[VMEM((QD // HD, 16, HD), jnp.float32)],
        compiler_params=pltpu.CompilerParams(vmem_limit_bytes=16 * MIB),
        cost_estimate=pl.CostEstimate(flops=2 * 16 * QD * WIDTH, bytes_accessed=2900000, transcendentals=0),
        name="final",
    )(attended, w_out.T)


def swap(x, axes):
    return lax.all_to_all(x, axes, 0, 0, tiled=True)


def body(
    embeddings, w_qkv, q_gain, w_out, parent_cache, parent_len, route, own_pool, own_table, own_len
):
    me = lax.axis_index(REP)
    parent = parent_cache.reshape(PSEGS, 2, BLK, KVH * HD)
    own = own_pool.reshape(4, 2, BLK, KVH * HD)
    def by_core(x):
        return lax.ppermute(x, "c", [(0, 1), (1, 0)])

    def by_x(x, d):
        return lax.ppermute(x, ("xl", "c"), [(i, i ^ d) for i in range(4)])

    def by_y(x, d):
        return lax.ppermute(x, ("y", "c"), [(i, i ^ d) for i in range(8)])

    def along(x, n):
        pairs = [
            (xl * 4 + y, (xl ^ (n % 2)) * 4 + (y + n) % 4) for xl in range(2) for y in range(4)
        ]
        return lax.ppermute(x, ("xl", "y"), pairs) if n else x

    barrier = lax.optimization_barrier
    sums, a2, b2, a3, b3, kv1 = start(embeddings, w_qkv, parent, own, own_table)
    a2, b2 = by_x(a2, 2), by_y(b2, 2)
    parts = swap(sums, TP)
    heads = norm_heads(parts, q_gain.reshape(1, HD))
    heads, a2, b2, a3, b3, kv1 = barrier((heads, a2, b2, a3, b3, kv1))
    a3, b3, kv1 = by_x(a3, 3), by_y(b3, 3), by_core(kv1)
    gathered = swap(heads, REP)
    gathered, a3, b3 = barrier((gathered, a3, b3))
    queries = [along(gathered, n) for n in range(4)]
    segs = lax.dynamic_index_in_dim(route, me, 1, keepdims=False)
    plen = lax.dynamic_index_in_dim(parent_len, me, 0, keepdims=True)
    partial = attend(
        segs, plen, own_len, own_table, parent, own, queries, (kv1, a2, b2, a3, b3)
    )
    folded = fold([along(partial[n], n) for n in range(4)])
    attended = merge(swap(folded, REP))
    everyone = swap(attended, TP)
    return final(everyone, w_out)


def solution(mesh):
    fine = Mesh(mesh.devices.reshape(8, 2, 2, 4, 2), ("z", "xh", "xl", "y", "c"))
    in_specs = (
        P(None, REP, TP),
        P(TP, None),
        P(),
        P(None, TP),
        P(REP, TP, None, None, None, None, None),
        P(),
        P(),
        P(REP, TP, None, None, None, None),
        P(REP, TP, None),
        P(REP, None),
    )
    out_specs = P(None, REP, TP)
    return jax.shard_map(body, mesh=fine, in_specs=in_specs, out_specs=out_specs, check_vma=False)
```

```python
import functools

import jax
import jax.numpy as jnp
from jax import lax
from jax.experimental import pallas as pl
from jax.experimental.pallas import tpu as pltpu
from jax.sharding import Mesh, PartitionSpec as P

HD = 128
BLK = 128
STEPS = 8
RPR = 2
KVH = 4
PSEGS = 8
N_REP = 16
N_TP = 16
WIDTH = 320
QD = 4096
CHUNK = 40
UNROLL = 16
START_MIB = 16

EPS = 1e-06
FAR = -1e30
SCALE2 = HD ** (-0.5) * 1.4426950408889634
MIB = 1024 * 1024

TP = ("xl", "y", "c")
REP = ("z", "xh")

VMEM = pltpu.VMEM
SMEM = pltpu.SMEM


def nt(a, b):
    return lax.dot_general(a, b, (((1,), (1,)), ((), ())), preferred_element_type=jnp.float32)


def lanes_of(head):
    return pl.ds(pl.multiple_of(head * HD, HD), HD)


def half_of(xl, y):
    return xl ^ (y % 2)


def start_kernel(emb_hbm, w, parent, own, table_hbm, sums, *rest):
    outs, (wide, emb, table, wsem, sem) = rest[0:5], rest[5:]
    c = lax.axis_index("c")
    h2 = half_of(lax.axis_index("xl"), lax.axis_index("y"))
    first = [
        pltpu.make_async_copy(table_hbm.at[0], table, wsem.at[5]),
        pltpu.make_async_copy(emb_hbm, emb, wsem.at[6]),
    ]
    loads = [
        pltpu.make_async_copy(
            w.at[:, pl.ds(n * 1024, 1024)], wide.at[:, pl.ds(n * 1024, 1024)], wsem.at[n]
        )
        for n in range(5)
    ]
    plans = [(2, 0, 4), (2, 4, 4), (3, 0, 4), (3, 4, 4), (1, 0, 8)]
    moves = []
    for n, (d, low, count) in enumerate(plans):
        lanes = lanes_of((h2 ^ (d // 2)) * 2 + (c ^ (d % 2)))
        moves.append(
            [
                pltpu.make_async_copy(
                    parent.at[pl.ds(low, count), :, :, lanes],
                    outs[n].at[pl.ds(0, count)],
                    sem.at[n, 0],
                )
            ]
        )
    for copy in first + loads + [copy for group in moves for copy in group]:
        copy.start()
    first[0].wait()
    for n, (d, low, count) in enumerate(plans):
        lanes = lanes_of((h2 ^ (d // 2)) * 2 + (c ^ (d % 2)))
        for i in range(count // 2):
            moves[n].append(
                pltpu.make_async_copy(
                    own.at[table[0, low // 2 + i], :, :, lanes],
                    outs[n].at[count + i],
                    sem.at[n, 1 + i],
                )
            )
            moves[n][-1].start()
    first[1].wait()
    rows = [emb[s].astype(jnp.float32) for s in range(STEPS)]
    flat = jnp.concatenate([rows[s][j : j + 1] for j in range(RPR) for s in range(STEPS)], axis=0)
    flat = flat.astype(jnp.bfloat16)
    for n in range(5):
        loads[n].wait()
        part = jnp.dot(
            flat, wide[:, n * 1024 : n * 1024 + 1024], preferred_element_type=jnp.float32
        )
        for k in range(KVH):
            for y in range(4):
                t = half_of(k // 2, y) * 8 + y * 2 + k % 2
                if n == k:
                    for j in range(RPR):
                        for g in range(2):
                            col = (2 * y + g) * HD
                            sums[t, j * 16 + g * 8 : j * 16 + g * 8 + 8, :] = part[
                                j * 8 : j * 8 + 8, col : col + HD
                            ]
                elif n == 4:
                    low = (y % 2) * 8 + (y // 2) * 4
                    sums[t, 32:40, :] = jnp.concatenate(
                        [
                            part[low : low + 4, col : col + HD]
                            for col in (k * HD, 512 + k * HD)
                        ],
                        axis=0,
                    )
    for group in moves:
        for copy in group:
            copy.wait()


def start(emb, w_qkv, parent, own, table):
    shapes = [(6, 2, BLK, HD)] * 4 + [(12, 2, BLK, HD)]
    return pl.pallas_call(
        start_kernel,
        in_specs=[pl.BlockSpec(memory_space=pltpu.HBM)] * 5,
        out_specs=[pl.BlockSpec(memory_space=VMEM)] * 6,
        out_shape=[jax.ShapeDtypeStruct((N_TP, CHUNK, HD), jnp.float32)]
        + [jax.ShapeDtypeStruct(shape, jnp.bfloat16) for shape in shapes],
        scratch_shapes=[
            VMEM((WIDTH, 5120), jnp.bfloat16),
            VMEM((STEPS, RPR, WIDTH), jnp.bfloat16),
            SMEM((1, 4), jnp.int32),
            pltpu.SemaphoreType.DMA((7,)),
            pltpu.SemaphoreType.DMA((5, 5)),
        ],
        compiler_params=pltpu.CompilerParams(vmem_limit_bytes=START_MIB * MIB),
        cost_estimate=pl.CostEstimate(flops=2 * 16 * WIDTH * 5120, bytes_accessed=9000000, transcendentals=0),
        name="start",
    )(*[pltpu.with_memory_space_constraint(a, pltpu.HBM) for a in (emb, w_qkv, parent, own, table)])


def norm_kernel(parts, gain, out, fresh):
    total = parts[0]
    for t in range(1, N_TP):
        total = total + parts[t]
    normed = total * lax.rsqrt(jnp.mean(total * total, axis=-1, keepdims=True) + EPS)
    result = (normed[0:32] * gain[...]).astype(jnp.bfloat16)
    for r in range(N_REP):
        out[r] = result
    row = lax.broadcasted_iota(jnp.int32, (8, HD), 0)
    tail = jnp.where(row < 4, normed[32:40], total[32:40])
    fresh[...] = tail.astype(jnp.bfloat16).astype(jnp.float32)


def norm_heads(parts, gain):
    return pl.pallas_call(
        norm_kernel,
        in_specs=[pl.BlockSpec(memory_space=VMEM)] * 2,
        out_specs=[pl.BlockSpec(memory_space=VMEM)] * 2,
        out_shape=[
            jax.ShapeDtypeStruct((N_REP, 32, HD), jnp.bfloat16),
            jax.ShapeDtypeStruct((8, HD), jnp.float32),
        ],
        compiler_params=pltpu.CompilerParams(vmem_limit_bytes=16 * MIB),
        cost_estimate=pl.CostEstimate(flops=400000, bytes_accessed=600000, transcendentals=64),
        name="norm_heads",
    )(parts, gain)


def gather_kernel(table, parent, own, kv1, a2, b2, a3, b3, keys, values, near, sem):
    xl = lax.axis_index("xl")
    y = lax.axis_index("y")
    c = lax.axis_index("c")
    lanes = lanes_of(half_of(xl, y) * 2 + c)
    loads = [
        pltpu.make_async_copy(parent.at[:, :, :, lanes], near.at[pl.ds(0, PSEGS)], sem.at[0])
    ] + [
        pltpu.make_async_copy(
            own.at[table[0, 0, e], :, :, lanes], near.at[PSEGS + e], sem.at[1 + e]
        )
        for e in range(4)
    ]
    for copy in loads:
        copy.start()
    for d, first, second in ((1, kv1, None), (2, a2, b2), (3, a3, b3), (0, near, None)):
        if d == 0:
            for copy in loads:
                copy.wait()
        for i in range(12):
            if second is None:
                piece, at = first, i
            elif i < PSEGS:
                piece, at = (first, i) if i < 4 else (second, i - 4)
            else:
                piece, at = (first, i - 4) if i < 10 else (second, i - 6)
            keys[d, i] = piece[at, 0]
            values[d, i] = piece[at, 1].T


def gather_cache(table, parent, own, pieces):
    return pl.pallas_call(
        gather_kernel,
        in_specs=[pl.BlockSpec(memory_space=SMEM)]
        + [pl.BlockSpec(memory_space=pltpu.HBM)] * 2
        + [pl.BlockSpec(memory_space=VMEM)] * 5,
        out_specs=[pl.BlockSpec(memory_space=VMEM)] * 2,
        out_shape=[jax.ShapeDtypeStruct((4, 12, BLK, HD), jnp.bfloat16)] * 2,
        scratch_shapes=[
            VMEM((12, 2, BLK, HD), jnp.bfloat16),
            pltpu.SemaphoreType.DMA((5,)),
        ],
        compiler_params=pltpu.CompilerParams(vmem_limit_bytes=16 * MIB),
        cost_estimate=pl.CostEstimate(flops=0, bytes_accessed=6000000, transcendentals=0),
        name="gather_cache",
    )(
        table,
        pltpu.with_memory_space_constraint(parent, pltpu.HBM),
        pltpu.with_memory_space_constraint(own, pltpu.HBM),
        *pieces,
    )


def soft(scores):
    top = jnp.max(scores, axis=0, keepdims=True)
    weights = jnp.exp2(scores - top)
    return top, jnp.sum(weights, axis=0, keepdims=True), weights.astype(jnp.bfloat16)


def split_level(level):
    high = level.astype(jnp.bfloat16).astype(jnp.float32)
    rest = level - high
    middle = rest.astype(jnp.bfloat16).astype(jnp.float32)
    return high, middle, rest - middle


def stat_rows(level):
    high, middle, low = split_level(level)
    row = lax.broadcasted_iota(jnp.int32, (8, HD), 0)
    return jnp.where(
        row == 0, high, jnp.where(row == 1, middle, jnp.where(row == 2, low, 0.0))
    )


def pair_queries(parts):
    zero = jnp.zeros((64, HD), jnp.bfloat16)
    q0 = jnp.concatenate([part[0:16] for part in parts], axis=0)
    q1 = jnp.concatenate([part[16:32] for part in parts], axis=0)
    return jnp.concatenate(
        [jnp.concatenate([q0, zero], axis=1), jnp.concatenate([zero, q1], axis=1)], axis=0
    )


def attend_kernel(segs, plen, olen, *refs):
    qin, (fresh, ks, vt), outs = refs[0:4], refs[4:7], refs[7:11]
    qs, save, levels = refs[11:14]
    xl = lax.axis_index("xl")
    y = lax.axis_index("y")
    c = lax.axis_index("c")
    me = lax.axis_index("z") * 2 + lax.axis_index("xh")
    owners = [(xl ^ (d // 2)) * 8 + y * 2 + (c ^ (d % 2)) for d in range(4)]
    owners_b = [xl * 8 + (y ^ (d // 2)) * 2 + (c ^ (d % 2)) for d in range(4)]
    left = lax.broadcasted_iota(jnp.int32, (1, HD), 1) < 64
    for n in range(4):
        qs[(y - n + 4) % 4] = qin[n][...]

    def emit(r, mixed, level):
        save[r] = mixed
        levels[pl.ds(r, 1), :] = level
        for n in range(4):
            part = save[r, pl.ds(pl.multiple_of(((y + n) % 4) * 32, 32), 32), :]
            outs[n][pl.ds(pl.multiple_of(r * 32, 32), 32), :] = part.astype(jnp.bfloat16)

    def one(r):
        s0 = segs[r, 0]
        s1 = segs[r, 1]
        keys = jnp.concatenate(
            [jnp.concatenate([ks[d, s0], ks[d, s1]], axis=1) for d in range(4)], axis=0
        )
        scores = nt(keys, pair_queries([qs[p, r] for p in range(4)])) * SCALE2
        limit = jnp.where(left, plen[0, s0], plen[0, s1])
        masked = []
        for d in range(4):
            owner = jnp.where(
                left,
                jnp.where(s0 < 4, owners[d], owners_b[d]),
                jnp.where(s1 < 4, owners[d], owners_b[d]),
            )
            masked.append(scores[d * BLK : d * BLK + BLK] + jnp.where(limit > owner, 0.0, FAR))
        top, total, weights = soft(jnp.concatenate(masked, axis=0))
        values = jnp.concatenate(
            [jnp.concatenate([vt[d, s] for d in range(4)], axis=1) for s in (s0, s1)], axis=0
        )
        both = jnp.dot(values, weights, preferred_element_type=jnp.float32)
        mixed = jnp.where(left, both[0:HD], both[HD : 2 * HD]) * (1.0 / total)
        emit(r, mixed, top + jnp.log2(total))

    def several(i, carry):
        for n in range(UNROLL):
            one(i * UNROLL + n)
        return carry

    lax.fori_loop(0, N_REP // UNROLL, several, 0)

    pad = jnp.zeros((BLK - 4, HD), jnp.float32)
    new_k = jnp.concatenate([fresh[0:4], pad], axis=0).astype(jnp.bfloat16)
    new_v = jnp.concatenate([fresh[4:8], pad], axis=0).T.astype(jnp.bfloat16)
    blocks = [(d, b) for d in range(4) for b in range(2)]
    keys = [jnp.concatenate([ks[d, 8 + b], ks[d, 10 + b]], axis=1) for d, b in blocks]
    keys.append(jnp.concatenate([new_k, new_k], axis=1))
    scores = nt(jnp.concatenate(keys, axis=0), pair_queries([qs[p, me] for p in range(4)])) * SCALE2
    limit = jnp.where(left, olen[0, 0], olen[0, 1])
    token = lax.broadcasted_iota(jnp.int32, (BLK, HD), 0)
    step = lax.broadcasted_iota(jnp.int32, (BLK, HD), 1) % 8
    masked = []
    for n, (d, b) in enumerate(blocks):
        owner = jnp.where(left, owners[d], owners_b[d])
        position = token + (b * N_TP + owner) * BLK
        masked.append(jnp.where(position < limit, scores[n * BLK : n * BLK + BLK], FAR))
    here = jnp.where(left, 0, 1) == y % 2
    known = (token < 4) & (token + (y // 2) * 4 <= step) & here
    masked.append(jnp.where(known, scores[8 * BLK : 9 * BLK], FAR))
    top, total, weights = soft(jnp.concatenate(masked, axis=0))
    values = jnp.concatenate(
        [
            jnp.concatenate(
                [vt[d, 8 + 2 * j + b] for d, b in blocks] + [new_v], axis=1
            )
            for j in range(2)
        ],
        axis=0,
    )
    both = jnp.dot(values, weights, preferred_element_type=jnp.float32)
    mixed = jnp.where(left, both[0:HD], both[HD : 2 * HD]) * (1.0 / total)
    level = top + jnp.log2(total)
    before = levels[pl.ds(me, 1), :]
    peak = jnp.maximum(before, level)
    scale_a = jnp.exp2(before - peak)
    scale_b = jnp.exp2(level - peak)
    total = scale_a + scale_b
    mixed = save[me] * (scale_a / total) + mixed * (scale_b / total)
    emit(me, mixed, peak + jnp.log2(total))
    tail = jnp.concatenate(split_level(levels[...]), axis=0).astype(jnp.bfloat16)
    for n in range(4):
        outs[n][pl.ds(N_REP * 32, 48), :] = tail


def attend(segs, plen, olen, queries, fresh, keys, values):
    return pl.pallas_call(
        attend_kernel,
        in_specs=[pl.BlockSpec(memory_space=SMEM)] * 3 + [pl.BlockSpec(memory_space=VMEM)] * 7,
        out_specs=[pl.BlockSpec(memory_space=VMEM)] * 4,
        out_shape=[jax.ShapeDtypeStruct((N_REP * 32 + 48, HD), jnp.bfloat16)] * 4,
        scratch_shapes=[
            VMEM((4, N_REP, 32, HD), jnp.bfloat16),
            VMEM((N_REP, HD, HD), jnp.float32),
            VMEM((N_REP, HD), jnp.float32),
        ],
        compiler_params=pltpu.CompilerParams(vmem_limit_bytes=24 * MIB),
        cost_estimate=pl.CostEstimate(flops=1600000000, bytes_accessed=4500000, transcendentals=1200000),
        name="attend",
    )(
        segs,
        plen,
        olen,
        *[pltpu.with_memory_space_constraint(part, VMEM) for part in (*queries, fresh, keys, values)],
    )


def level_of(part):
    return jnp.sum(part[32:40].astype(jnp.float32), axis=0, keepdims=True)


def fold_kernel(p0, p1, p2, p3, out, shares, tops):
    refs = (p0, p1, p2, p3)
    levels = []
    for p in refs:
        tail = p[pl.ds(N_REP * 32, 48), :].astype(jnp.float32)
        levels.append(tail[0:16] + tail[16:32] + tail[32:48])
    top = jnp.maximum(jnp.maximum(levels[0], levels[1]), jnp.maximum(levels[2], levels[3]))
    weights = [jnp.exp2(level - top) for level in levels]
    total = (weights[0] + weights[1]) + (weights[2] + weights[3])
    share = 1.0 / total
    for n in range(4):
        shares[n] = weights[n] * share
    tops[...] = top + jnp.log2(total)

    def one(r, carry):
        mixed = jnp.zeros((32, HD), jnp.float32)
        for n, p in enumerate(refs):
            part = p[pl.ds(pl.multiple_of(r * 32, 32), 32), :].astype(jnp.float32)
            mixed = mixed + part * shares[n, pl.ds(r, 1), :]
        out[r] = jnp.concatenate([mixed, stat_rows(tops[pl.ds(r, 1), :])], axis=0).astype(
            jnp.bfloat16
        )
        return carry

    lax.fori_loop(0, N_REP, one, 0, unroll=4)


def fold(parts):
    return pl.pallas_call(
        fold_kernel,
        in_specs=[pl.BlockSpec(memory_space=VMEM)] * 4,
        out_specs=pl.BlockSpec(memory_space=VMEM),
        out_shape=jax.ShapeDtypeStruct((N_REP, CHUNK, HD), jnp.bfloat16),
        scratch_shapes=[VMEM((4, N_REP, HD), jnp.float32), VMEM((N_REP, HD), jnp.float32)],
        compiler_params=pltpu.CompilerParams(vmem_limit_bytes=16 * MIB),
        cost_estimate=pl.CostEstimate(flops=1000000, bytes_accessed=800000, transcendentals=8192),
        name="fold_blocks",
    )(*parts)


def merge_kernel(parts, out):
    level = jnp.concatenate([level_of(parts[i]) for i in range(N_REP)], axis=0)
    weight = jnp.exp2(level - jnp.max(level, axis=0, keepdims=True))
    weight = weight * (1.0 / jnp.sum(weight, axis=0, keepdims=True))
    total = jnp.zeros((32, HD), jnp.float32)
    for i in range(N_REP):
        total = total + parts[i, 0:32, :].astype(jnp.float32) * weight[i : i + 1]
    result = total.astype(jnp.bfloat16)
    for t in range(N_TP):
        out[t] = result


def merge(parts):
    return pl.pallas_call(
        merge_kernel,
        in_specs=[pl.BlockSpec(memory_space=VMEM)],
        out_specs=pl.BlockSpec(memory_space=VMEM),
        out_shape=jax.ShapeDtypeStruct((N_TP, 32, HD), jnp.bfloat16),
        compiler_params=pltpu.CompilerParams(vmem_limit_bytes=16 * MIB),
        cost_estimate=pl.CostEstimate(flops=200000, bytes_accessed=300000, transcendentals=2048),
        name="merge_owners",
    )(parts)


def final_kernel(attended, w_out, out, rows):
    for k in range(KVH):
        tile = jnp.concatenate(
            [
                attended[half_of(k // 2, p) * 8 + p * 2 + k % 2].astype(jnp.float32)
                for p in range(4)
            ],
            axis=0,
        )
        turned = tile.T
        for j in range(RPR):
            for g in range(8):
                rows[k * 8 + g, pl.ds(j, 8, stride=2), :] = turned[
                    j * 64 + g * 8 : j * 64 + g * 8 + 8
                ]
    wide = jnp.concatenate([rows[h].astype(jnp.bfloat16) for h in range(QD // HD)], axis=1)
    result = nt(wide, w_out[...])
    for s in range(STEPS):
        out[s] = result[2 * s : 2 * s + 2].astype(jnp.bfloat16)


def final(attended, w_out):
    return pl.pallas_call(
        final_kernel,
        in_specs=[pl.BlockSpec(memory_space=VMEM)] * 2,
        out_specs=pl.BlockSpec(memory_space=VMEM),
        out_shape=jax.ShapeDtypeStruct((STEPS, RPR, WIDTH), jnp.bfloat16),
        scratch_shapes=[VMEM((QD // HD, 16, HD), jnp.float32)],
        compiler_params=pltpu.CompilerParams(vmem_limit_bytes=16 * MIB),
        cost_estimate=pl.CostEstimate(flops=2 * 16 * QD * WIDTH, bytes_accessed=2900000, transcendentals=0),
        name="final",
    )(attended, w_out.T)


def swap(x, axes):
    return lax.all_to_all(x, axes, 0, 0, tiled=True)


def body(
    embeddings, w_qkv, q_gain, w_out, parent_cache, parent_len, route, own_pool, own_table, own_len
):
    me = lax.axis_index(REP)
    parent = parent_cache.reshape(PSEGS, 2, BLK, KVH * HD)
    own = own_pool.reshape(4, 2, BLK, KVH * HD)
    def by_core(x):
        return lax.ppermute(x, "c", [(0, 1), (1, 0)])

    def by_x(x, d):
        return lax.ppermute(x, ("xl", "c"), [(i, i ^ d) for i in range(4)])

    def by_y(x, d):
        return lax.ppermute(x, ("y", "c"), [(i, i ^ d) for i in range(8)])

    def along(x, n):
        pairs = [
            (xl * 4 + y, (xl ^ (n % 2)) * 4 + (y + n) % 4) for xl in range(2) for y in range(4)
        ]
        return lax.ppermute(x, ("xl", "y"), pairs) if n else x

    barrier = lax.optimization_barrier
    sums, a2, b2, a3, b3, kv1 = start(embeddings, w_qkv, parent, own, own_table)
    a2, b2 = by_x(a2, 2), by_y(b2, 2)
    parts = swap(sums, TP)
    heads, fresh = norm_heads(parts, q_gain.reshape(1, HD))
    heads, a2, b2, a3, b3, kv1 = barrier((heads, a2, b2, a3, b3, kv1))
    a3, b3, kv1 = by_x(a3, 3), by_y(b3, 3), by_core(kv1)
    gathered = swap(heads, REP)
    gathered, a3, b3, parent = barrier((gathered, a3, b3, parent))
    queries = [along(gathered, n) for n in range(4)]
    keys, values = gather_cache(own_table, parent, own, (kv1, a2, b2, a3, b3))
    segs = lax.dynamic_index_in_dim(route, me, 1, keepdims=False)
    plen = lax.dynamic_index_in_dim(parent_len, me, 0, keepdims=True)
    partial = attend(segs, plen, own_len, queries, fresh, keys, values)
    folded = fold([along(partial[n], n) for n in range(4)])
    attended = merge(swap(folded, REP))
    everyone = swap(attended, TP)
    return final(everyone, w_out)


def solution(mesh):
    fine = Mesh(mesh.devices.reshape(8, 2, 2, 4, 2), ("z", "xh", "xl", "y", "c"))
    in_specs = (
        P(None, REP, TP),
        P(TP, None),
        P(),
        P(None, TP),
        P(REP, TP, None, None, None, None, None),
        P(),
        P(),
        P(REP, TP, None, None, None, None),
        P(REP, TP, None),
        P(REP, None),
    )
    out_specs = P(None, REP, TP)
    return jax.shard_map(body, mesh=fine, in_specs=in_specs, out_specs=out_specs, check_vma=False)
```

```python
import functools

import jax
import jax.numpy as jnp
from jax import lax
from jax.experimental import pallas as pl
from jax.experimental.pallas import tpu as pltpu
from jax.sharding import Mesh, PartitionSpec as P

HD = 128
BLK = 128
STEPS = 8
RPR = 2
KVH = 4
PSEGS = 8
N_REP = 16
N_TP = 16
WIDTH = 320
QD = 4096
CHUNK = 40
UNROLL = 16
START_MIB = 16

EPS = 1e-06
FAR = -1e30
SCALE2 = HD ** (-0.5) * 1.4426950408889634
MIB = 1024 * 1024

TP = ("xl", "y", "c")
REP = ("z", "xh")

VMEM = pltpu.VMEM
SMEM = pltpu.SMEM


def nt(a, b):
    return lax.dot_general(a, b, (((1,), (1,)), ((), ())), preferred_element_type=jnp.float32)


def lanes_of(head):
    return pl.ds(pl.multiple_of(head * HD, HD), HD)


def half_of(xl, y):
    return xl ^ (y % 2)


def start_kernel(emb_hbm, w, parent, own, table_hbm, mine, other, *rest):
    outs, (wide, emb, table, sums, wsem, sem) = rest[0:5], rest[5:]
    c = lax.axis_index("c")
    h2 = half_of(lax.axis_index("xl"), lax.axis_index("y"))
    first = [
        pltpu.make_async_copy(table_hbm.at[0], table, wsem.at[5]),
        pltpu.make_async_copy(emb_hbm, emb, wsem.at[6]),
    ]
    loads = [
        pltpu.make_async_copy(
            w.at[:, pl.ds(n * 1024, 1024)], wide.at[:, pl.ds(n * 1024, 1024)], wsem.at[n]
        )
        for n in range(5)
    ]
    plans = [(2, 0, 4), (2, 4, 4), (3, 0, 4), (3, 4, 4), (1, 0, 8)]
    moves = []
    for n, (d, low, count) in enumerate(plans):
        lanes = lanes_of((h2 ^ (d // 2)) * 2 + (c ^ (d % 2)))
        moves.append(
            [
                pltpu.make_async_copy(
                    parent.at[pl.ds(low, count), :, :, lanes],
                    outs[n].at[pl.ds(0, count)],
                    sem.at[n, 0],
                )
            ]
        )
    for copy in first + loads + [copy for group in moves for copy in group]:
        copy.start()
    first[0].wait()
    for n, (d, low, count) in enumerate(plans):
        lanes = lanes_of((h2 ^ (d // 2)) * 2 + (c ^ (d % 2)))
        for i in range(count // 2):
            moves[n].append(
                pltpu.make_async_copy(
                    own.at[table[0, low // 2 + i], :, :, lanes],
                    outs[n].at[count + i],
                    sem.at[n, 1 + i],
                )
            )
            moves[n][-1].start()
    first[1].wait()
    rows = [emb[s].astype(jnp.float32) for s in range(STEPS)]
    flat = jnp.concatenate([rows[s][j : j + 1] for j in range(RPR) for s in range(STEPS)], axis=0)
    flat = flat.astype(jnp.bfloat16)
    for n in range(5):
        loads[n].wait()
        part = jnp.dot(
            flat, wide[:, n * 1024 : n * 1024 + 1024], preferred_element_type=jnp.float32
        )
        for k in range(KVH):
            for y in range(4):
                t = half_of(k // 2, y) * 4 + y
                side = (k % 2) ^ c
                if n == k:
                    for j in range(RPR):
                        for g in range(2):
                            col = (2 * y + g) * HD
                            sums[side, t, j * 16 + g * 8 : j * 16 + g * 8 + 8, :] = part[
                                j * 8 : j * 8 + 8, col : col + HD
                            ]
                elif n == 4:
                    low = (y % 2) * 8 + (y // 2) * 4
                    sums[side, t, 32:40, :] = jnp.concatenate(
                        [
                            part[low : low + 4, col : col + HD]
                            for col in (k * HD, 512 + k * HD)
                        ],
                        axis=0,
                    )
    mine[...] = sums[0]
    other[...] = sums[1]
    for group in moves:
        for copy in group:
            copy.wait()


def start(emb, w_qkv, parent, own, table):
    shapes = [(6, 2, BLK, HD)] * 4 + [(12, 2, BLK, HD)]
    return pl.pallas_call(
        start_kernel,
        in_specs=[pl.BlockSpec(memory_space=pltpu.HBM)] * 5,
        out_specs=[pl.BlockSpec(memory_space=VMEM)] * 7,
        out_shape=[jax.ShapeDtypeStruct((8, CHUNK, HD), jnp.float32)] * 2
        + [jax.ShapeDtypeStruct(shape, jnp.bfloat16) for shape in shapes],
        scratch_shapes=[
            VMEM((WIDTH, 5120), jnp.bfloat16),
            VMEM((STEPS, RPR, WIDTH), jnp.bfloat16),
            SMEM((1, 4), jnp.int32),
            VMEM((2, 8, CHUNK, HD), jnp.float32),
            pltpu.SemaphoreType.DMA((7,)),
            pltpu.SemaphoreType.DMA((5, 5)),
        ],
        compiler_params=pltpu.CompilerParams(vmem_limit_bytes=START_MIB * MIB),
        cost_estimate=pl.CostEstimate(flops=2 * 16 * WIDTH * 5120, bytes_accessed=9000000, transcendentals=0),
        name="start",
    )(*[pltpu.with_memory_space_constraint(a, pltpu.HBM) for a in (emb, w_qkv, parent, own, table)])


def add_kernel(a, b, out):
    out[...] = a[...] + b[...]


def add(a, b):
    return pl.pallas_call(
        add_kernel,
        in_specs=[pl.BlockSpec(memory_space=VMEM)] * 2,
        out_specs=pl.BlockSpec(memory_space=VMEM),
        out_shape=jax.ShapeDtypeStruct(a.shape, a.dtype),
        compiler_params=pltpu.CompilerParams(vmem_limit_bytes=16 * MIB),
        cost_estimate=pl.CostEstimate(flops=40960, bytes_accessed=500000, transcendentals=0),
        name="add_cores",
    )(a, b)


def norm_kernel(parts, gain, out, fresh):
    total = parts[0]
    for t in range(1, 8):
        total = total + parts[t]
    normed = total * lax.rsqrt(jnp.mean(total * total, axis=-1, keepdims=True) + EPS)
    result = (normed[0:32] * gain[...]).astype(jnp.bfloat16)
    for r in range(N_REP):
        out[r] = result
    row = lax.broadcasted_iota(jnp.int32, (8, HD), 0)
    tail = jnp.where(row < 4, normed[32:40], total[32:40])
    fresh[...] = tail.astype(jnp.bfloat16).astype(jnp.float32)


def norm_heads(parts, gain):
    return pl.pallas_call(
        norm_kernel,
        in_specs=[pl.BlockSpec(memory_space=VMEM)] * 2,
        out_specs=[pl.BlockSpec(memory_space=VMEM)] * 2,
        out_shape=[
            jax.ShapeDtypeStruct((N_REP, 32, HD), jnp.bfloat16),
            jax.ShapeDtypeStruct((8, HD), jnp.float32),
        ],
        compiler_params=pltpu.CompilerParams(vmem_limit_bytes=16 * MIB),
        cost_estimate=pl.CostEstimate(flops=400000, bytes_accessed=600000, transcendentals=64),
        name="norm_heads",
    )(parts, gain)


def gather_kernel(table, parent, own, kv1, a2, b2, a3, b3, keys, values, near, sem):
    xl = lax.axis_index("xl")
    y = lax.axis_index("y")
    c = lax.axis_index("c")
    lanes = lanes_of(half_of(xl, y) * 2 + c)
    loads = [
        pltpu.make_async_copy(parent.at[:, :, :, lanes], near.at[pl.ds(0, PSEGS)], sem.at[0])
    ] + [
        pltpu.make_async_copy(
            own.at[table[0, 0, e], :, :, lanes], near.at[PSEGS + e], sem.at[1 + e]
        )
        for e in range(4)
    ]
    for copy in loads:
        copy.start()
    for d, first, second in ((1, kv1, None), (2, a2, b2), (3, a3, b3), (0, near, None)):
        if d == 0:
            for copy in loads:
                copy.wait()
        for i in range(12):
            if second is None:
                piece, at = first, i
            elif i < PSEGS:
                piece, at = (first, i) if i < 4 else (second, i - 4)
            else:
                piece, at = (first, i - 4) if i < 10 else (second, i - 6)
            keys[d, i] = piece[at, 0]
            values[d, i] = piece[at, 1].T


def gather_cache(table, parent, own, pieces):
    return pl.pallas_call(
        gather_kernel,
        in_specs=[pl.BlockSpec(memory_space=SMEM)]
        + [pl.BlockSpec(memory_space=pltpu.HBM)] * 2
        + [pl.BlockSpec(memory_space=VMEM)] * 5,
        out_specs=[pl.BlockSpec(memory_space=VMEM)] * 2,
        out_shape=[jax.ShapeDtypeStruct((4, 12, BLK, HD), jnp.bfloat16)] * 2,
        scratch_shapes=[
            VMEM((12, 2, BLK, HD), jnp.bfloat16),
            pltpu.SemaphoreType.DMA((5,)),
        ],
        compiler_params=pltpu.CompilerParams(vmem_limit_bytes=16 * MIB),
        cost_estimate=pl.CostEstimate(flops=0, bytes_accessed=6000000, transcendentals=0),
        name="gather_cache",
    )(
        table,
        pltpu.with_memory_space_constraint(parent, pltpu.HBM),
        pltpu.with_memory_space_constraint(own, pltpu.HBM),
        *pieces,
    )


def soft(scores):
    top = jnp.max(scores, axis=0, keepdims=True)
    weights = jnp.exp2(scores - top)
    return top, jnp.sum(weights, axis=0, keepdims=True), weights.astype(jnp.bfloat16)


def split_level(level):
    high = level.astype(jnp.bfloat16).astype(jnp.float32)
    rest = level - high
    middle = rest.astype(jnp.bfloat16).astype(jnp.float32)
    return high, middle, rest - middle


def stat_rows(level):
    high, middle, low = split_level(level)
    row = lax.broadcasted_iota(jnp.int32, (8, HD), 0)
    return jnp.where(
        row == 0, high, jnp.where(row == 1, middle, jnp.where(row == 2, low, 0.0))
    )


def pair_queries(parts):
    zero = jnp.zeros((64, HD), jnp.bfloat16)
    q0 = jnp.concatenate([part[0:16] for part in parts], axis=0)
    q1 = jnp.concatenate([part[16:32] for part in parts], axis=0)
    return jnp.concatenate(
        [jnp.concatenate([q0, zero], axis=1), jnp.concatenate([zero, q1], axis=1)], axis=0
    )


def attend_kernel(segs, plen, olen, *refs):
    qin, (fresh, ks, vt), outs = refs[0:4], refs[4:7], refs[7:11]
    qs, save, levels = refs[11:14]
    xl = lax.axis_index("xl")
    y = lax.axis_index("y")
    c = lax.axis_index("c")
    me = lax.axis_index("z") * 2 + lax.axis_index("xh")
    owners = [(xl ^ (d // 2)) * 8 + y * 2 + (c ^ (d % 2)) for d in range(4)]
    owners_b = [xl * 8 + (y ^ (d // 2)) * 2 + (c ^ (d % 2)) for d in range(4)]
    left = lax.broadcasted_iota(jnp.int32, (1, HD), 1) < 64
    for n in range(4):
        qs[(y - n + 4) % 4] = qin[n][...]

    def emit(r, mixed, level):
        save[r] = mixed
        levels[pl.ds(r, 1), :] = level
        for n in range(4):
            part = save[r, pl.ds(pl.multiple_of(((y + n) % 4) * 32, 32), 32), :]
            outs[n][pl.ds(pl.multiple_of(r * 32, 32), 32), :] = part.astype(jnp.bfloat16)

    def one(r):
        s0 = segs[r, 0]
        s1 = segs[r, 1]
        keys = jnp.concatenate(
            [jnp.concatenate([ks[d, s0], ks[d, s1]], axis=1) for d in range(4)], axis=0
        )
        scores = nt(keys, pair_queries([qs[p, r] for p in range(4)])) * SCALE2
        limit = jnp.where(left, plen[0, s0], plen[0, s1])
        masked = []
        for d in range(4):
            owner = jnp.where(
                left,
                jnp.where(s0 < 4, owners[d], owners_b[d]),
                jnp.where(s1 < 4, owners[d], owners_b[d]),
            )
            masked.append(scores[d * BLK : d * BLK + BLK] + jnp.where(limit > owner, 0.0, FAR))
        top, total, weights = soft(jnp.concatenate(masked, axis=0))
        values = jnp.concatenate(
            [jnp.concatenate([vt[d, s] for d in range(4)], axis=1) for s in (s0, s1)], axis=0
        )
        both = jnp.dot(values, weights, preferred_element_type=jnp.float32)
        mixed = jnp.where(left, both[0:HD], both[HD : 2 * HD]) * (1.0 / total)
        emit(r, mixed, top + jnp.log2(total))

    def several(i, carry):
        for n in range(UNROLL):
            one(i * UNROLL + n)
        return carry

    lax.fori_loop(0, N_REP // UNROLL, several, 0)

    pad = jnp.zeros((BLK - 4, HD), jnp.float32)
    new_k = jnp.concatenate([fresh[0:4], pad], axis=0).astype(jnp.bfloat16)
    new_v = jnp.concatenate([fresh[4:8], pad], axis=0).T.astype(jnp.bfloat16)
    blocks = [(d, b) for d in range(4) for b in range(2)]
    keys = [jnp.concatenate([ks[d, 8 + b], ks[d, 10 + b]], axis=1) for d, b in blocks]
    keys.append(jnp.concatenate([new_k, new_k], axis=1))
    scores = nt(jnp.concatenate(keys, axis=0), pair_queries([qs[p, me] for p in range(4)])) * SCALE2
    limit = jnp.where(left, olen[0, 0], olen[0, 1])
    token = lax.broadcasted_iota(jnp.int32, (BLK, HD), 0)
    step = lax.broadcasted_iota(jnp.int32, (BLK, HD), 1) % 8
    masked = []
    for n, (d, b) in enumerate(blocks):
        owner = jnp.where(left, owners[d], owners_b[d])
        position = token + (b * N_TP + owner) * BLK
        masked.append(jnp.where(position < limit, scores[n * BLK : n * BLK + BLK], FAR))
    here = jnp.where(left, 0, 1) == y % 2
    known = (token < 4) & (token + (y // 2) * 4 <= step) & here
    masked.append(jnp.where(known, scores[8 * BLK : 9 * BLK], FAR))
    top, total, weights = soft(jnp.concatenate(masked, axis=0))
    values = jnp.concatenate(
        [
            jnp.concatenate(
                [vt[d, 8 + 2 * j + b] for d, b in blocks] + [new_v], axis=1
            )
            for j in range(2)
        ],
        axis=0,
    )
    both = jnp.dot(values, weights, preferred_element_type=jnp.float32)
    mixed = jnp.where(left, both[0:HD], both[HD : 2 * HD]) * (1.0 / total)
    level = top + jnp.log2(total)
    before = levels[pl.ds(me, 1), :]
    peak = jnp.maximum(before, level)
    scale_a = jnp.exp2(before - peak)
    scale_b = jnp.exp2(level - peak)
    total = scale_a + scale_b
    mixed = save[me] * (scale_a / total) + mixed * (scale_b / total)
    emit(me, mixed, peak + jnp.log2(total))
    tail = jnp.concatenate(split_level(levels[...]), axis=0).astype(jnp.bfloat16)
    for n in range(4):
        outs[n][pl.ds(N_REP * 32, 48), :] = tail


def attend(segs, plen, olen, queries, fresh, keys, values):
    return pl.pallas_call(
        attend_kernel,
        in_specs=[pl.BlockSpec(memory_space=SMEM)] * 3 + [pl.BlockSpec(memory_space=VMEM)] * 7,
        out_specs=[pl.BlockSpec(memory_space=VMEM)] * 4,
        out_shape=[jax.ShapeDtypeStruct((N_REP * 32 + 48, HD), jnp.bfloat16)] * 4,
        scratch_shapes=[
            VMEM((4, N_REP, 32, HD), jnp.bfloat16),
            VMEM((N_REP, HD, HD), jnp.float32),
            VMEM((N_REP, HD), jnp.float32),
        ],
        compiler_params=pltpu.CompilerParams(vmem_limit_bytes=24 * MIB),
        cost_estimate=pl.CostEstimate(flops=1600000000, bytes_accessed=4500000, transcendentals=1200000),
        name="attend",
    )(
        segs,
        plen,
        olen,
        *[pltpu.with_memory_space_constraint(part, VMEM) for part in (*queries, fresh, keys, values)],
    )


def level_of(part):
    return jnp.sum(part[32:40].astype(jnp.float32), axis=0, keepdims=True)


def fold_kernel(p0, p1, p2, p3, out, shares, tops):
    refs = (p0, p1, p2, p3)
    levels = []
    for p in refs:
        tail = p[pl.ds(N_REP * 32, 48), :].astype(jnp.float32)
        levels.append(tail[0:16] + tail[16:32] + tail[32:48])
    top = jnp.maximum(jnp.maximum(levels[0], levels[1]), jnp.maximum(levels[2], levels[3]))
    weights = [jnp.exp2(level - top) for level in levels]
    total = (weights[0] + weights[1]) + (weights[2] + weights[3])
    share = 1.0 / total
    for n in range(4):
        shares[n] = weights[n] * share
    tops[...] = top + jnp.log2(total)

    def one(r, carry):
        mixed = jnp.zeros((32, HD), jnp.float32)
        for n, p in enumerate(refs):
            part = p[pl.ds(pl.multiple_of(r * 32, 32), 32), :].astype(jnp.float32)
            mixed = mixed + part * shares[n, pl.ds(r, 1), :]
        out[r] = jnp.concatenate([mixed, stat_rows(tops[pl.ds(r, 1), :])], axis=0).astype(
            jnp.bfloat16
        )
        return carry

    lax.fori_loop(0, N_REP, one, 0, unroll=4)


def fold(parts):
    return pl.pallas_call(
        fold_kernel,
        in_specs=[pl.BlockSpec(memory_space=VMEM)] * 4,
        out_specs=pl.BlockSpec(memory_space=VMEM),
        out_shape=jax.ShapeDtypeStruct((N_REP, CHUNK, HD), jnp.bfloat16),
        scratch_shapes=[VMEM((4, N_REP, HD), jnp.float32), VMEM((N_REP, HD), jnp.float32)],
        compiler_params=pltpu.CompilerParams(vmem_limit_bytes=16 * MIB),
        cost_estimate=pl.CostEstimate(flops=1000000, bytes_accessed=800000, transcendentals=8192),
        name="fold_blocks",
    )(*parts)


def merge_kernel(parts, out):
    level = jnp.concatenate([level_of(parts[i]) for i in range(N_REP)], axis=0)
    weight = jnp.exp2(level - jnp.max(level, axis=0, keepdims=True))
    weight = weight * (1.0 / jnp.sum(weight, axis=0, keepdims=True))
    total = jnp.zeros((32, HD), jnp.float32)
    for i in range(N_REP):
        total = total + parts[i, 0:32, :].astype(jnp.float32) * weight[i : i + 1]
    result = total.astype(jnp.bfloat16)
    for t in range(N_TP):
        out[t] = result


def merge(parts):
    return pl.pallas_call(
        merge_kernel,
        in_specs=[pl.BlockSpec(memory_space=VMEM)],
        out_specs=pl.BlockSpec(memory_space=VMEM),
        out_shape=jax.ShapeDtypeStruct((N_TP, 32, HD), jnp.bfloat16),
        compiler_params=pltpu.CompilerParams(vmem_limit_bytes=16 * MIB),
        cost_estimate=pl.CostEstimate(flops=200000, bytes_accessed=300000, transcendentals=2048),
        name="merge_owners",
    )(parts)


def final_kernel(attended, w_out, out, rows):
    for k in range(KVH):
        tile = jnp.concatenate(
            [
                attended[half_of(k // 2, p) * 8 + p * 2 + k % 2].astype(jnp.float32)
                for p in range(4)
            ],
            axis=0,
        )
        turned = tile.T
        for j in range(RPR):
            for g in range(8):
                rows[k * 8 + g, pl.ds(j, 8, stride=2), :] = turned[
                    j * 64 + g * 8 : j * 64 + g * 8 + 8
                ]
    wide = jnp.concatenate([rows[h].astype(jnp.bfloat16) for h in range(QD // HD)], axis=1)
    result = nt(wide, w_out[...])
    for s in range(STEPS):
        out[s] = result[2 * s : 2 * s + 2].astype(jnp.bfloat16)


def final(attended, w_out):
    return pl.pallas_call(
        final_kernel,
        in_specs=[pl.BlockSpec(memory_space=VMEM)] * 2,
        out_specs=pl.BlockSpec(memory_space=VMEM),
        out_shape=jax.ShapeDtypeStruct((STEPS, RPR, WIDTH), jnp.bfloat16),
        scratch_shapes=[VMEM((QD // HD, 16, HD), jnp.float32)],
        compiler_params=pltpu.CompilerParams(vmem_limit_bytes=16 * MIB),
        cost_estimate=pl.CostEstimate(flops=2 * 16 * QD * WIDTH, bytes_accessed=2900000, transcendentals=0),
        name="final",
    )(attended, w_out.T)


def swap(x, axes):
    return lax.all_to_all(x, axes, 0, 0, tiled=True)


def body(
    embeddings, w_qkv, q_gain, w_out, parent_cache, parent_len, route, own_pool, own_table, own_len
):
    me = lax.axis_index(REP)
    parent = parent_cache.reshape(PSEGS, 2, BLK, KVH * HD)
    own = own_pool.reshape(4, 2, BLK, KVH * HD)
    def by_core(x):
        return lax.ppermute(x, "c", [(0, 1), (1, 0)])

    def by_x(x, d):
        return lax.ppermute(x, ("xl", "c"), [(i, i ^ d) for i in range(4)])

    def by_y(x, d):
        return lax.ppermute(x, ("y", "c"), [(i, i ^ d) for i in range(8)])

    def along(x, n):
        pairs = [
            (xl * 4 + y, (xl ^ (n % 2)) * 4 + (y + n) % 4) for xl in range(2) for y in range(4)
        ]
        return lax.ppermute(x, ("xl", "y"), pairs) if n else x

    barrier = lax.optimization_barrier
    mine, other, a2, b2, a3, b3, kv1 = start(embeddings, w_qkv, parent, own, own_table)
    other = by_core(other)
    a2, b2 = by_x(a2, 2), by_y(b2, 2)
    parts = swap(add(mine, other), ("xl", "y"))
    heads, fresh = norm_heads(parts, q_gain.reshape(1, HD))
    heads, a2, b2, a3, b3, kv1 = barrier((heads, a2, b2, a3, b3, kv1))
    a3, b3, kv1 = by_x(a3, 3), by_y(b3, 3), by_core(kv1)
    gathered = swap(heads, REP)
    gathered, a3, b3, parent = barrier((gathered, a3, b3, parent))
    queries = [along(gathered, n) for n in range(4)]
    keys, values = gather_cache(own_table, parent, own, (kv1, a2, b2, a3, b3))
    segs = lax.dynamic_index_in_dim(route, me, 1, keepdims=False)
    plen = lax.dynamic_index_in_dim(parent_len, me, 0, keepdims=True)
    partial = attend(segs, plen, own_len, queries, fresh, keys, values)
    folded = fold([along(partial[n], n) for n in range(4)])
    attended = merge(swap(folded, REP))
    everyone = swap(attended, TP)
    return final(everyone, w_out)


def solution(mesh):
    fine = Mesh(mesh.devices.reshape(8, 2, 2, 4, 2), ("z", "xh", "xl", "y", "c"))
    in_specs = (
        P(None, REP, TP),
        P(TP, None),
        P(),
        P(None, TP),
        P(REP, TP, None, None, None, None, None),
        P(),
        P(),
        P(REP, TP, None, None, None, None),
        P(REP, TP, None),
        P(REP, None),
    )
    out_specs = P(None, REP, TP)
    return jax.shard_map(body, mesh=fine, in_specs=in_specs, out_specs=out_specs, check_vma=False)
```

```python
import functools

import jax
import jax.numpy as jnp
from jax import lax
from jax.experimental import pallas as pl
from jax.experimental.pallas import tpu as pltpu
from jax.sharding import Mesh, PartitionSpec as P

HD = 128
BLK = 128
STEPS = 8
RPR = 2
KVH = 4
PSEGS = 8
N_REP = 16
N_TP = 16
WIDTH = 320
QD = 4096
CHUNK = 40
UNROLL = 16
START_MIB = 16

EPS = 1e-06
FAR = -1e30
SCALE2 = HD ** (-0.5) * 1.4426950408889634
MIB = 1024 * 1024

TP = ("xl", "y", "c")
REP = ("z", "xh")

VMEM = pltpu.VMEM
SMEM = pltpu.SMEM


def nt(a, b):
    return lax.dot_general(a, b, (((1,), (1,)), ((), ())), preferred_element_type=jnp.float32)


def lanes_of(head):
    return pl.ds(pl.multiple_of(head * HD, HD), HD)


def half_of(xl, y):
    return xl ^ (y % 2)


PLANS = ((2, 0, 4), (2, 4, 4), (3, 0, 4), (3, 4, 4), (1, 0, 4), (1, 4, 4))


def cut_copies(plans, parent, own, table, outs, sem):
    c = lax.axis_index("c")
    h2 = half_of(lax.axis_index("xl"), lax.axis_index("y"))
    lanes = [lanes_of((h2 ^ (d // 2)) * 2 + (c ^ (d % 2))) for d, _, _ in plans]
    moves = [
        pltpu.make_async_copy(
            parent.at[pl.ds(low, count), :, :, lanes[n]],
            outs[n].at[pl.ds(0, count)],
            sem.at[n, 0],
        )
        for n, (_, low, count) in enumerate(plans)
    ]

    def late():
        return [
            pltpu.make_async_copy(
                own.at[table[0, low // 2 + i], :, :, lanes[n]],
                outs[n].at[count + i],
                sem.at[n, 1 + i],
            )
            for n, (_, low, count) in enumerate(plans)
            for i in range(count // 2)
        ]

    return moves, late


def cut_kernel(parent, own, table_hbm, *rest):
    outs, (table, tsem, sem) = rest[0:4], rest[4:]
    first = pltpu.make_async_copy(table_hbm.at[0], table, tsem)
    first.start()
    moves, late = cut_copies(PLANS[2:], parent, own, table, outs, sem)
    for copy in moves:
        copy.start()
    first.wait()
    late = late()
    for copy in late:
        copy.start()
    for copy in moves + late:
        copy.wait()


def cut_rest(parent, own, table):
    return pl.pallas_call(
        cut_kernel,
        in_specs=[pl.BlockSpec(memory_space=pltpu.HBM)] * 3,
        out_specs=[pl.BlockSpec(memory_space=VMEM)] * 4,
        out_shape=[jax.ShapeDtypeStruct((6, 2, BLK, HD), jnp.bfloat16)] * 4,
        scratch_shapes=[
            SMEM((1, 4), jnp.int32),
            pltpu.SemaphoreType.DMA,
            pltpu.SemaphoreType.DMA((4, 5)),
        ],
        compiler_params=pltpu.CompilerParams(vmem_limit_bytes=16 * MIB),
        cost_estimate=pl.CostEstimate(flops=0, bytes_accessed=3000000, transcendentals=0),
        name="cut_rest",
    )(*[pltpu.with_memory_space_constraint(a, pltpu.HBM) for a in (parent, own, table)])


def start_kernel(emb_hbm, w, parent, own, table_hbm, mine, other, *rest):
    outs, (wide, emb, table, sums, wsem, sem) = rest[0:2], rest[2:]
    c = lax.axis_index("c")
    first = [
        pltpu.make_async_copy(table_hbm.at[0], table, wsem.at[5]),
        pltpu.make_async_copy(emb_hbm, emb, wsem.at[6]),
    ]
    loads = [
        pltpu.make_async_copy(
            w.at[:, pl.ds(n * 1024, 1024)], wide.at[:, pl.ds(n * 1024, 1024)], wsem.at[n]
        )
        for n in range(5)
    ]
    moves, late = cut_copies(PLANS[:2], parent, own, table, outs, sem)
    for copy in first + loads + moves:
        copy.start()
    first[0].wait()
    late = late()
    for copy in late:
        copy.start()
    first[1].wait()
    rows = [emb[s].astype(jnp.float32) for s in range(STEPS)]
    flat = jnp.concatenate([rows[s][j : j + 1] for j in range(RPR) for s in range(STEPS)], axis=0)
    flat = flat.astype(jnp.bfloat16)
    for n in range(5):
        loads[n].wait()
        part = jnp.dot(
            flat, wide[:, n * 1024 : n * 1024 + 1024], preferred_element_type=jnp.float32
        )
        for k in range(KVH):
            for y in range(4):
                t = half_of(k // 2, y) * 4 + y
                side = (k % 2) ^ c
                if n == k:
                    for j in range(RPR):
                        for g in range(2):
                            col = (2 * y + g) * HD
                            sums[side, t, j * 16 + g * 8 : j * 16 + g * 8 + 8, :] = part[
                                j * 8 : j * 8 + 8, col : col + HD
                            ]
                elif n == 4:
                    low = (y % 2) * 8 + (y // 2) * 4
                    sums[side, t, 32:40, :] = jnp.concatenate(
                        [
                            part[low : low + 4, col : col + HD]
                            for col in (k * HD, 512 + k * HD)
                        ],
                        axis=0,
                    )
    mine[...] = sums[0]
    other[...] = sums[1]
    for copy in moves + late:
        copy.wait()


def start(emb, w_qkv, parent, own, table):
    piece = jax.ShapeDtypeStruct((6, 2, BLK, HD), jnp.bfloat16)
    return pl.pallas_call(
        start_kernel,
        in_specs=[pl.BlockSpec(memory_space=pltpu.HBM)] * 5,
        out_specs=[pl.BlockSpec(memory_space=VMEM)] * 4,
        out_shape=[jax.ShapeDtypeStruct((8, CHUNK, HD), jnp.float32)] * 2
        + [piece] * 2,
        scratch_shapes=[
            VMEM((WIDTH, 5120), jnp.bfloat16),
            VMEM((STEPS, RPR, WIDTH), jnp.bfloat16),
            SMEM((1, 4), jnp.int32),
            VMEM((2, 8, CHUNK, HD), jnp.float32),
            pltpu.SemaphoreType.DMA((7,)),
            pltpu.SemaphoreType.DMA((2, 5)),
        ],
        compiler_params=pltpu.CompilerParams(vmem_limit_bytes=START_MIB * MIB),
        cost_estimate=pl.CostEstimate(flops=2 * 16 * WIDTH * 5120, bytes_accessed=9000000, transcendentals=0),
        name="start",
    )(*[pltpu.with_memory_space_constraint(a, pltpu.HBM) for a in (emb, w_qkv, parent, own, table)])


def add_kernel(a, b, out):
    out[...] = a[...] + b[...]


def add(a, b):
    return pl.pallas_call(
        add_kernel,
        in_specs=[pl.BlockSpec(memory_space=VMEM)] * 2,
        out_specs=pl.BlockSpec(memory_space=VMEM),
        out_shape=jax.ShapeDtypeStruct(a.shape, a.dtype),
        compiler_params=pltpu.CompilerParams(vmem_limit_bytes=16 * MIB),
        cost_estimate=pl.CostEstimate(flops=40960, bytes_accessed=500000, transcendentals=0),
        name="add_cores",
    )(a, b)


def norm_kernel(parts, gain, out, fresh):
    total = parts[0]
    for t in range(1, 8):
        total = total + parts[t]
    normed = total * lax.rsqrt(jnp.mean(total * total, axis=-1, keepdims=True) + EPS)
    result = (normed[0:32] * gain[...]).astype(jnp.bfloat16)
    for r in range(N_REP):
        out[r] = result
    row = lax.broadcasted_iota(jnp.int32, (8, HD), 0)
    tail = jnp.where(row < 4, normed[32:40], total[32:40])
    fresh[...] = tail.astype(jnp.bfloat16).astype(jnp.float32)


def norm_heads(parts, gain):
    return pl.pallas_call(
        norm_kernel,
        in_specs=[pl.BlockSpec(memory_space=VMEM)] * 2,
        out_specs=[pl.BlockSpec(memory_space=VMEM)] * 2,
        out_shape=[
            jax.ShapeDtypeStruct((N_REP, 32, HD), jnp.bfloat16),
            jax.ShapeDtypeStruct((8, HD), jnp.float32),
        ],
        compiler_params=pltpu.CompilerParams(vmem_limit_bytes=16 * MIB),
        cost_estimate=pl.CostEstimate(flops=400000, bytes_accessed=600000, transcendentals=64),
        name="norm_heads",
    )(parts, gain)


def gather_kernel(table, parent, own, a1, b1, a2, b2, a3, b3, keys, values, near, sem):
    xl = lax.axis_index("xl")
    y = lax.axis_index("y")
    c = lax.axis_index("c")
    lanes = lanes_of(half_of(xl, y) * 2 + c)
    loads = [
        pltpu.make_async_copy(parent.at[:, :, :, lanes], near.at[pl.ds(0, PSEGS)], sem.at[0])
    ] + [
        pltpu.make_async_copy(
            own.at[table[0, 0, e], :, :, lanes], near.at[PSEGS + e], sem.at[1 + e]
        )
        for e in range(4)
    ]
    for copy in loads:
        copy.start()
    for d, first, second in ((1, a1, b1), (2, a2, b2), (3, a3, b3), (0, near, None)):
        if d == 0:
            for copy in loads:
                copy.wait()
        for i in range(12):
            if second is None:
                piece, at = first, i
            elif i < PSEGS:
                piece, at = (first, i) if i < 4 else (second, i - 4)
            else:
                piece, at = (first, i - 4) if i < 10 else (second, i - 6)
            keys[d, i] = piece[at, 0]
            values[d, i] = piece[at, 1].T


def gather_cache(table, parent, own, pieces):
    return pl.pallas_call(
        gather_kernel,
        in_specs=[pl.BlockSpec(memory_space=SMEM)]
        + [pl.BlockSpec(memory_space=pltpu.HBM)] * 2
        + [pl.BlockSpec(memory_space=VMEM)] * 6,
        out_specs=[pl.BlockSpec(memory_space=VMEM)] * 2,
        out_shape=[jax.ShapeDtypeStruct((4, 12, BLK, HD), jnp.bfloat16)] * 2,
        scratch_shapes=[
            VMEM((12, 2, BLK, HD), jnp.bfloat16),
            pltpu.SemaphoreType.DMA((5,)),
        ],
        compiler_params=pltpu.CompilerParams(vmem_limit_bytes=16 * MIB),
        cost_estimate=pl.CostEstimate(flops=0, bytes_accessed=6000000, transcendentals=0),
        name="gather_cache",
    )(
        table,
        pltpu.with_memory_space_constraint(parent, pltpu.HBM),
        pltpu.with_memory_space_constraint(own, pltpu.HBM),
        *pieces,
    )


def soft(scores):
    top = jnp.max(scores, axis=0, keepdims=True)
    weights = jnp.exp2(scores - top)
    return top, jnp.sum(weights, axis=0, keepdims=True), weights.astype(jnp.bfloat16)


def split_level(level):
    high = level.astype(jnp.bfloat16).astype(jnp.float32)
    rest = level - high
    middle = rest.astype(jnp.bfloat16).astype(jnp.float32)
    return high, middle, rest - middle


def stat_rows(level):
    high, middle, low = split_level(level)
    row = lax.broadcasted_iota(jnp.int32, (8, HD), 0)
    return jnp.where(
        row == 0, high, jnp.where(row == 1, middle, jnp.where(row == 2, low, 0.0))
    )


def pair_queries(parts):
    zero = jnp.zeros((64, HD), jnp.bfloat16)
    q0 = jnp.concatenate([part[0:16] for part in parts], axis=0)
    q1 = jnp.concatenate([part[16:32] for part in parts], axis=0)
    return jnp.concatenate(
        [jnp.concatenate([q0, zero], axis=1), jnp.concatenate([zero, q1], axis=1)], axis=0
    )


def attend_kernel(segs, plen, olen, *refs):
    qin, (fresh, ks, vt), outs = refs[0:4], refs[4:7], refs[7:11]
    qs, save, levels = refs[11:14]
    xl = lax.axis_index("xl")
    y = lax.axis_index("y")
    c = lax.axis_index("c")
    me = lax.axis_index("z") * 2 + lax.axis_index("xh")
    owners = [(xl ^ (d // 2)) * 8 + y * 2 + (c ^ (d % 2)) for d in range(4)]
    owners_b = [xl * 8 + (y ^ (d // 2)) * 2 + (c ^ (d % 2)) for d in range(4)]
    left = lax.broadcasted_iota(jnp.int32, (1, HD), 1) < 64
    for n in range(4):
        qs[(y - n + 4) % 4] = qin[n][...]

    def emit(r, mixed, level):
        save[r] = mixed
        levels[pl.ds(r, 1), :] = level
        for n in range(4):
            part = save[r, pl.ds(pl.multiple_of(((y + n) % 4) * 32, 32), 32), :]
            outs[n][pl.ds(pl.multiple_of(r * 32, 32), 32), :] = part.astype(jnp.bfloat16)

    def one(r):
        s0 = segs[r, 0]
        s1 = segs[r, 1]
        keys = jnp.concatenate(
            [jnp.concatenate([ks[d, s0], ks[d, s1]], axis=1) for d in range(4)], axis=0
        )
        scores = nt(keys, pair_queries([qs[p, r] for p in range(4)])) * SCALE2
        limit = jnp.where(left, plen[0, s0], plen[0, s1])
        masked = []
        for d in range(4):
            owner = jnp.where(
                left,
                jnp.where(s0 < 4, owners[d], owners_b[d]),
                jnp.where(s1 < 4, owners[d], owners_b[d]),
            )
            masked.append(scores[d * BLK : d * BLK + BLK] + jnp.where(limit > owner, 0.0, FAR))
        top, total, weights = soft(jnp.concatenate(masked, axis=0))
        values = jnp.concatenate(
            [jnp.concatenate([vt[d, s] for d in range(4)], axis=1) for s in (s0, s1)], axis=0
        )
        both = jnp.dot(values, weights, preferred_element_type=jnp.float32)
        mixed = jnp.where(left, both[0:HD], both[HD : 2 * HD]) * (1.0 / total)
        emit(r, mixed, top + jnp.log2(total))

    def several(i, carry):
        for n in range(UNROLL):
            one(i * UNROLL + n)
        return carry

    lax.fori_loop(0, N_REP // UNROLL, several, 0)

    pad = jnp.zeros((BLK - 4, HD), jnp.float32)
    new_k = jnp.concatenate([fresh[0:4], pad], axis=0).astype(jnp.bfloat16)
    new_v = jnp.concatenate([fresh[4:8], pad], axis=0).T.astype(jnp.bfloat16)
    blocks = [(d, b) for d in range(4) for b in range(2)]
    keys = [jnp.concatenate([ks[d, 8 + b], ks[d, 10 + b]], axis=1) for d, b in blocks]
    keys.append(jnp.concatenate([new_k, new_k], axis=1))
    scores = nt(jnp.concatenate(keys, axis=0), pair_queries([qs[p, me] for p in range(4)])) * SCALE2
    limit = jnp.where(left, olen[0, 0], olen[0, 1])
    token = lax.broadcasted_iota(jnp.int32, (BLK, HD), 0)
    step = lax.broadcasted_iota(jnp.int32, (BLK, HD), 1) % 8
    masked = []
    for n, (d, b) in enumerate(blocks):
        owner = jnp.where(left, owners[d], owners_b[d])
        position = token + (b * N_TP + owner) * BLK
        masked.append(jnp.where(position < limit, scores[n * BLK : n * BLK + BLK], FAR))
    here = jnp.where(left, 0, 1) == y % 2
    known = (token < 4) & (token + (y // 2) * 4 <= step) & here
    masked.append(jnp.where(known, scores[8 * BLK : 9 * BLK], FAR))
    top, total, weights = soft(jnp.concatenate(masked, axis=0))
    values = jnp.concatenate(
        [
            jnp.concatenate(
                [vt[d, 8 + 2 * j + b] for d, b in blocks] + [new_v], axis=1
            )
            for j in range(2)
        ],
        axis=0,
    )
    both = jnp.dot(values, weights, preferred_element_type=jnp.float32)
    mixed = jnp.where(left, both[0:HD], both[HD : 2 * HD]) * (1.0 / total)
    level = top + jnp.log2(total)
    before = levels[pl.ds(me, 1), :]
    peak = jnp.maximum(before, level)
    scale_a = jnp.exp2(before - peak)
    scale_b = jnp.exp2(level - peak)
    total = scale_a + scale_b
    mixed = save[me] * (scale_a / total) + mixed * (scale_b / total)
    emit(me, mixed, peak + jnp.log2(total))
    tail = jnp.concatenate(split_level(levels[...]), axis=0).astype(jnp.bfloat16)
    for n in range(4):
        outs[n][pl.ds(N_REP * 32, 48), :] = tail


def attend(segs, plen, olen, queries, fresh, keys, values):
    return pl.pallas_call(
        attend_kernel,
        in_specs=[pl.BlockSpec(memory_space=SMEM)] * 3 + [pl.BlockSpec(memory_space=VMEM)] * 7,
        out_specs=[pl.BlockSpec(memory_space=VMEM)] * 4,
        out_shape=[jax.ShapeDtypeStruct((N_REP * 32 + 48, HD), jnp.bfloat16)] * 4,
        scratch_shapes=[
            VMEM((4, N_REP, 32, HD), jnp.bfloat16),
            VMEM((N_REP, HD, HD), jnp.float32),
            VMEM((N_REP, HD), jnp.float32),
        ],
        compiler_params=pltpu.CompilerParams(vmem_limit_bytes=24 * MIB),
        cost_estimate=pl.CostEstimate(flops=1600000000, bytes_accessed=4500000, transcendentals=1200000),
        name="attend",
    )(
        segs,
        plen,
        olen,
        *[pltpu.with_memory_space_constraint(part, VMEM) for part in (*queries, fresh, keys, values)],
    )


def level_of(part):
    return jnp.sum(part[32:40].astype(jnp.float32), axis=0, keepdims=True)


def fold_kernel(p0, p1, p2, p3, out, shares, tops):
    refs = (p0, p1, p2, p3)
    levels = []
    for p in refs:
        tail = p[pl.ds(N_REP * 32, 48), :].astype(jnp.float32)
        levels.append(tail[0:16] + tail[16:32] + tail[32:48])
    top = jnp.maximum(jnp.maximum(levels[0], levels[1]), jnp.maximum(levels[2], levels[3]))
    weights = [jnp.exp2(level - top) for level in levels]
    total = (weights[0] + weights[1]) + (weights[2] + weights[3])
    share = 1.0 / total
    for n in range(4):
        shares[n] = weights[n] * share
    tops[...] = top + jnp.log2(total)

    def one(r, carry):
        mixed = jnp.zeros((32, HD), jnp.float32)
        for n, p in enumerate(refs):
            part = p[pl.ds(pl.multiple_of(r * 32, 32), 32), :].astype(jnp.float32)
            mixed = mixed + part * shares[n, pl.ds(r, 1), :]
        out[r] = jnp.concatenate([mixed, stat_rows(tops[pl.ds(r, 1), :])], axis=0).astype(
            jnp.bfloat16
        )
        return carry

    lax.fori_loop(0, N_REP, one, 0, unroll=4)


def fold(parts):
    return pl.pallas_call(
        fold_kernel,
        in_specs=[pl.BlockSpec(memory_space=VMEM)] * 4,
        out_specs=pl.BlockSpec(memory_space=VMEM),
        out_shape=jax.ShapeDtypeStruct((N_REP, CHUNK, HD), jnp.bfloat16),
        scratch_shapes=[VMEM((4, N_REP, HD), jnp.float32), VMEM((N_REP, HD), jnp.float32)],
        compiler_params=pltpu.CompilerParams(vmem_limit_bytes=16 * MIB),
        cost_estimate=pl.CostEstimate(flops=1000000, bytes_accessed=800000, transcendentals=8192),
        name="fold_blocks",
    )(*parts)


def merge_kernel(parts, out):
    level = jnp.concatenate([level_of(parts[i]) for i in range(N_REP)], axis=0)
    weight = jnp.exp2(level - jnp.max(level, axis=0, keepdims=True))
    weight = weight * (1.0 / jnp.sum(weight, axis=0, keepdims=True))
    total = jnp.zeros((32, HD), jnp.float32)
    for i in range(N_REP):
        total = total + parts[i, 0:32, :].astype(jnp.float32) * weight[i : i + 1]
    result = total.astype(jnp.bfloat16)
    for t in range(N_TP):
        out[t] = result


def merge(parts):
    return pl.pallas_call(
        merge_kernel,
        in_specs=[pl.BlockSpec(memory_space=VMEM)],
        out_specs=pl.BlockSpec(memory_space=VMEM),
        out_shape=jax.ShapeDtypeStruct((N_TP, 32, HD), jnp.bfloat16),
        compiler_params=pltpu.CompilerParams(vmem_limit_bytes=16 * MIB),
        cost_estimate=pl.CostEstimate(flops=200000, bytes_accessed=300000, transcendentals=2048),
        name="merge_owners",
    )(parts)


def final_kernel(attended, w_out, out, rows):
    for k in range(KVH):
        tile = jnp.concatenate(
            [
                attended[half_of(k // 2, p) * 8 + p * 2 + k % 2].astype(jnp.float32)
                for p in range(4)
            ],
            axis=0,
        )
        turned = tile.T
        for j in range(RPR):
            for g in range(8):
                rows[k * 8 + g, pl.ds(j, 8, stride=2), :] = turned[
                    j * 64 + g * 8 : j * 64 + g * 8 + 8
                ]
    wide = jnp.concatenate([rows[h].astype(jnp.bfloat16) for h in range(QD // HD)], axis=1)
    result = nt(wide, w_out[...])
    for s in range(STEPS):
        out[s] = result[2 * s : 2 * s + 2].astype(jnp.bfloat16)


def final(attended, w_out):
    return pl.pallas_call(
        final_kernel,
        in_specs=[pl.BlockSpec(memory_space=VMEM)] * 2,
        out_specs=pl.BlockSpec(memory_space=VMEM),
        out_shape=jax.ShapeDtypeStruct((STEPS, RPR, WIDTH), jnp.bfloat16),
        scratch_shapes=[VMEM((QD // HD, 16, HD), jnp.float32)],
        compiler_params=pltpu.CompilerParams(vmem_limit_bytes=16 * MIB),
        cost_estimate=pl.CostEstimate(flops=2 * 16 * QD * WIDTH, bytes_accessed=2900000, transcendentals=0),
        name="final",
    )(attended, w_out.T)


def swap(x, axes):
    return lax.all_to_all(x, axes, 0, 0, tiled=True)


def body(
    embeddings, w_qkv, q_gain, w_out, parent_cache, parent_len, route, own_pool, own_table, own_len
):
    me = lax.axis_index(REP)
    parent = parent_cache.reshape(PSEGS, 2, BLK, KVH * HD)
    own = own_pool.reshape(4, 2, BLK, KVH * HD)
    def by_core(x):
        return lax.ppermute(x, "c", [(0, 1), (1, 0)])

    def by_x(x, d):
        return lax.ppermute(x, ("xl", "c"), [(i, i ^ d) for i in range(4)])

    def by_y(x, d):
        return lax.ppermute(x, ("y", "c"), [(i, i ^ d) for i in range(8)])

    def along(x, n):
        pairs = [
            (xl * 4 + y, (xl ^ (n % 2)) * 4 + (y + n) % 4) for xl in range(2) for y in range(4)
        ]
        return lax.ppermute(x, ("xl", "y"), pairs) if n else x

    barrier = lax.optimization_barrier
    mine, other, a2, b2 = start(embeddings, w_qkv, parent, own, own_table)
    a3, b3, a1, b1 = cut_rest(parent, own, own_table)
    other = by_core(other)
    a2, b2 = by_x(a2, 2), by_y(b2, 2)
    parts = swap(add(mine, other), ("xl", "y"))
    parts, a3, b3, a1, b1 = barrier((parts, a3, b3, a1, b1))
    heads, fresh = norm_heads(parts, q_gain.reshape(1, HD))
    heads, a2, b2, a3, b3, a1, b1 = barrier((heads, a2, b2, a3, b3, a1, b1))
    a3, b3, a1, b1 = by_x(a3, 3), by_y(b3, 3), by_core(a1), by_core(b1)
    gathered = swap(heads, REP)
    gathered, a3, b3, parent = barrier((gathered, a3, b3, parent))
    queries = [along(gathered, n) for n in range(4)]
    keys, values = gather_cache(own_table, parent, own, (a1, b1, a2, b2, a3, b3))
    segs = lax.dynamic_index_in_dim(route, me, 1, keepdims=False)
    plen = lax.dynamic_index_in_dim(parent_len, me, 0, keepdims=True)
    partial = attend(segs, plen, own_len, queries, fresh, keys, values)
    folded = fold([along(partial[n], n) for n in range(4)])
    attended = merge(swap(folded, REP))
    everyone = swap(attended, TP)
    return final(everyone, w_out)


def solution(mesh):
    fine = Mesh(mesh.devices.reshape(8, 2, 2, 4, 2), ("z", "xh", "xl", "y", "c"))
    in_specs = (
        P(None, REP, TP),
        P(TP, None),
        P(),
        P(None, TP),
        P(REP, TP, None, None, None, None, None),
        P(),
        P(),
        P(REP, TP, None, None, None, None),
        P(REP, TP, None),
        P(REP, None),
    )
    out_specs = P(None, REP, TP)
    return jax.shard_map(body, mesh=fine, in_specs=in_specs, out_specs=out_specs, check_vma=False)
```

```python
import functools

import jax
import jax.numpy as jnp
from jax import lax
from jax.experimental import pallas as pl
from jax.experimental.pallas import tpu as pltpu
from jax.sharding import Mesh, PartitionSpec as P

HD = 128
BLK = 128
STEPS = 8
RPR = 2
KVH = 4
PSEGS = 8
N_REP = 16
N_TP = 16
WIDTH = 320
QD = 4096
CHUNK = 40
UNROLL = 16
START_MIB = 16

EPS = 1e-06
FAR = -1e30
SCALE2 = HD ** (-0.5) * 1.4426950408889634
MIB = 1024 * 1024

TP = ("xl", "y", "c")
REP = ("z", "xh")

VMEM = pltpu.VMEM
SMEM = pltpu.SMEM


def nt(a, b):
    return lax.dot_general(a, b, (((1,), (1,)), ((), ())), preferred_element_type=jnp.float32)


def lanes_of(head):
    return pl.ds(pl.multiple_of(head * HD, HD), HD)


def half_of(xl, y):
    return xl ^ (y % 2)


PLANS = ((2, 0, 4), (2, 4, 4), (3, 0, 4), (3, 4, 4), (1, 0, 4), (1, 4, 4))


def cut_copies(plans, parent, own, table, outs, sem):
    c = lax.axis_index("c")
    h2 = half_of(lax.axis_index("xl"), lax.axis_index("y"))
    lanes = [lanes_of((h2 ^ (d // 2)) * 2 + (c ^ (d % 2))) for d, _, _ in plans]
    moves = [
        pltpu.make_async_copy(
            parent.at[pl.ds(low, count), :, :, lanes[n]],
            outs[n].at[pl.ds(0, count)],
            sem.at[n, 0],
        )
        for n, (_, low, count) in enumerate(plans)
    ]

    def late():
        return [
            pltpu.make_async_copy(
                own.at[table[0, low // 2 + i], :, :, lanes[n]],
                outs[n].at[count + i],
                sem.at[n, 1 + i],
            )
            for n, (_, low, count) in enumerate(plans)
            for i in range(count // 2)
        ]

    return moves, late


def cut_kernel(parent, own, table_hbm, *rest):
    outs, (table, tsem, sem) = rest[0:4], rest[4:]
    first = pltpu.make_async_copy(table_hbm.at[0], table, tsem)
    first.start()
    moves, late = cut_copies(PLANS[2:], parent, own, table, outs, sem)
    for copy in moves:
        copy.start()
    first.wait()
    late = late()
    for copy in late:
        copy.start()
    for copy in moves + late:
        copy.wait()


def cut_rest(parent, own, table):
    return pl.pallas_call(
        cut_kernel,
        in_specs=[pl.BlockSpec(memory_space=pltpu.HBM)] * 3,
        out_specs=[pl.BlockSpec(memory_space=VMEM)] * 4,
        out_shape=[jax.ShapeDtypeStruct((6, 2, BLK, HD), jnp.bfloat16)] * 4,
        scratch_shapes=[
            SMEM((1, 4), jnp.int32),
            pltpu.SemaphoreType.DMA,
            pltpu.SemaphoreType.DMA((4, 5)),
        ],
        compiler_params=pltpu.CompilerParams(vmem_limit_bytes=16 * MIB),
        cost_estimate=pl.CostEstimate(flops=0, bytes_accessed=3000000, transcendentals=0),
        name="cut_rest",
    )(*[pltpu.with_memory_space_constraint(a, pltpu.HBM) for a in (parent, own, table)])


def start_kernel(emb_hbm, w, parent, own, table_hbm, mine, other, *rest):
    outs, (wide, emb, table, sums, wsem, sem) = rest[0:2], rest[2:]
    c = lax.axis_index("c")
    first = [
        pltpu.make_async_copy(table_hbm.at[0], table, wsem.at[5]),
        pltpu.make_async_copy(emb_hbm, emb, wsem.at[6]),
    ]
    loads = [
        pltpu.make_async_copy(
            w.at[:, pl.ds(n * 1024, 1024)], wide.at[:, pl.ds(n * 1024, 1024)], wsem.at[n]
        )
        for n in range(5)
    ]
    moves, late = cut_copies(PLANS[:2], parent, own, table, outs, sem)
    for copy in first + loads + moves:
        copy.start()
    first[0].wait()
    late = late()
    for copy in late:
        copy.start()
    first[1].wait()
    rows = [emb[s].astype(jnp.float32) for s in range(STEPS)]
    flat = jnp.concatenate([rows[s][j : j + 1] for j in range(RPR) for s in range(STEPS)], axis=0)
    flat = flat.astype(jnp.bfloat16)
    for n in range(5):
        loads[n].wait()
        part = jnp.dot(
            flat, wide[:, n * 1024 : n * 1024 + 1024], preferred_element_type=jnp.float32
        )
        for k in range(KVH):
            for y in range(4):
                t = half_of(k // 2, y) * 4 + y
                side = (k % 2) ^ c
                if n == k:
                    for j in range(RPR):
                        for g in range(2):
                            col = (2 * y + g) * HD
                            sums[side, t, j * 16 + g * 8 : j * 16 + g * 8 + 8, :] = part[
                                j * 8 : j * 8 + 8, col : col + HD
                            ]
                elif n == 4:
                    low = (y % 2) * 8 + (y // 2) * 4
                    sums[side, t, 32:40, :] = jnp.concatenate(
                        [
                            part[low : low + 4, col : col + HD]
                            for col in (k * HD, 512 + k * HD)
                        ],
                        axis=0,
                    )
    mine[...] = sums[0]
    other[...] = sums[1]
    for copy in moves + late:
        copy.wait()


def start(emb, w_qkv, parent, own, table):
    piece = jax.ShapeDtypeStruct((6, 2, BLK, HD), jnp.bfloat16)
    return pl.pallas_call(
        start_kernel,
        in_specs=[pl.BlockSpec(memory_space=pltpu.HBM)] * 5,
        out_specs=[pl.BlockSpec(memory_space=VMEM)] * 4,
        out_shape=[jax.ShapeDtypeStruct((8, CHUNK, HD), jnp.float32)] * 2
        + [piece] * 2,
        scratch_shapes=[
            VMEM((WIDTH, 5120), jnp.bfloat16),
            VMEM((STEPS, RPR, WIDTH), jnp.bfloat16),
            SMEM((1, 4), jnp.int32),
            VMEM((2, 8, CHUNK, HD), jnp.float32),
            pltpu.SemaphoreType.DMA((7,)),
            pltpu.SemaphoreType.DMA((2, 5)),
        ],
        compiler_params=pltpu.CompilerParams(vmem_limit_bytes=START_MIB * MIB),
        cost_estimate=pl.CostEstimate(flops=2 * 16 * WIDTH * 5120, bytes_accessed=9000000, transcendentals=0),
        name="start",
    )(*[pltpu.with_memory_space_constraint(a, pltpu.HBM) for a in (emb, w_qkv, parent, own, table)])


def add_kernel(a, b, out):
    out[...] = a[...] + b[...]


def add(a, b):
    return pl.pallas_call(
        add_kernel,
        in_specs=[pl.BlockSpec(memory_space=VMEM)] * 2,
        out_specs=pl.BlockSpec(memory_space=VMEM),
        out_shape=jax.ShapeDtypeStruct(a.shape, a.dtype),
        compiler_params=pltpu.CompilerParams(vmem_limit_bytes=16 * MIB),
        cost_estimate=pl.CostEstimate(flops=40960, bytes_accessed=500000, transcendentals=0),
        name="add_cores",
    )(a, b)


def norm_kernel(parts, gain, out, fresh):
    total = parts[0]
    for t in range(1, 8):
        total = total + parts[t]
    normed = total * lax.rsqrt(jnp.mean(total * total, axis=-1, keepdims=True) + EPS)
    result = (normed[0:32] * gain[...]).astype(jnp.bfloat16)
    for r in range(N_REP):
        out[r] = result
    row = lax.broadcasted_iota(jnp.int32, (8, HD), 0)
    tail = jnp.where(row < 4, normed[32:40], total[32:40])
    fresh[...] = tail.astype(jnp.bfloat16).astype(jnp.float32)


def norm_heads(parts, gain):
    return pl.pallas_call(
        norm_kernel,
        in_specs=[pl.BlockSpec(memory_space=VMEM)] * 2,
        out_specs=[pl.BlockSpec(memory_space=VMEM)] * 2,
        out_shape=[
            jax.ShapeDtypeStruct((N_REP, 32, HD), jnp.bfloat16),
            jax.ShapeDtypeStruct((8, HD), jnp.float32),
        ],
        compiler_params=pltpu.CompilerParams(vmem_limit_bytes=16 * MIB),
        cost_estimate=pl.CostEstimate(flops=400000, bytes_accessed=600000, transcendentals=64),
        name="norm_heads",
    )(parts, gain)


def gather_kernel(table, parent, own, a1, b1, a2, b2, a3, b3, keys, values, near, sem):
    xl = lax.axis_index("xl")
    y = lax.axis_index("y")
    c = lax.axis_index("c")
    lanes = lanes_of(half_of(xl, y) * 2 + c)
    loads = [
        pltpu.make_async_copy(parent.at[:, :, :, lanes], near.at[pl.ds(0, PSEGS)], sem.at[0])
    ] + [
        pltpu.make_async_copy(
            own.at[table[0, 0, e], :, :, lanes], near.at[PSEGS + e], sem.at[1 + e]
        )
        for e in range(4)
    ]
    for copy in loads:
        copy.start()
    for d, first, second in ((1, a1, b1), (2, a2, b2), (3, a3, b3), (0, near, None)):
        if d == 0:
            for copy in loads:
                copy.wait()
        for i in range(12):
            if second is None:
                piece, at = first, i
            elif i < PSEGS:
                piece, at = (first, i) if i < 4 else (second, i - 4)
            else:
                piece, at = (first, i - 4) if i < 10 else (second, i - 6)
            keys[d, i] = piece[at, 0]
            values[d, i] = piece[at, 1].T


def gather_cache(table, parent, own, pieces):
    return pl.pallas_call(
        gather_kernel,
        in_specs=[pl.BlockSpec(memory_space=SMEM)]
        + [pl.BlockSpec(memory_space=pltpu.HBM)] * 2
        + [pl.BlockSpec(memory_space=VMEM)] * 6,
        out_specs=[pl.BlockSpec(memory_space=VMEM)] * 2,
        out_shape=[jax.ShapeDtypeStruct((4, 12, BLK, HD), jnp.bfloat16)] * 2,
        scratch_shapes=[
            VMEM((12, 2, BLK, HD), jnp.bfloat16),
            pltpu.SemaphoreType.DMA((5,)),
        ],
        compiler_params=pltpu.CompilerParams(vmem_limit_bytes=16 * MIB),
        cost_estimate=pl.CostEstimate(flops=0, bytes_accessed=6000000, transcendentals=0),
        name="gather_cache",
    )(
        table,
        pltpu.with_memory_space_constraint(parent, pltpu.HBM),
        pltpu.with_memory_space_constraint(own, pltpu.HBM),
        *pieces,
    )


def soft(scores):
    top = jnp.max(scores, axis=0, keepdims=True)
    weights = jnp.exp2(scores - top)
    return top, jnp.sum(weights, axis=0, keepdims=True), weights.astype(jnp.bfloat16)


def split_level(level):
    high = level.astype(jnp.bfloat16).astype(jnp.float32)
    rest = level - high
    middle = rest.astype(jnp.bfloat16).astype(jnp.float32)
    return high, middle, rest - middle


def stat_rows(level):
    high, middle, low = split_level(level)
    row = lax.broadcasted_iota(jnp.int32, (8, HD), 0)
    return jnp.where(
        row == 0, high, jnp.where(row == 1, middle, jnp.where(row == 2, low, 0.0))
    )


def pair_queries(parts):
    zero = jnp.zeros((64, HD), jnp.bfloat16)
    q0 = jnp.concatenate([part[0:16] for part in parts], axis=0)
    q1 = jnp.concatenate([part[16:32] for part in parts], axis=0)
    return jnp.concatenate(
        [jnp.concatenate([q0, zero], axis=1), jnp.concatenate([zero, q1], axis=1)], axis=0
    )


def attend_kernel(segs, plen, olen, *refs):
    qin, (fresh, ks, vt), outs = refs[0:4], refs[4:7], refs[7:11]
    qs, save, levels = refs[11:14]
    xl = lax.axis_index("xl")
    y = lax.axis_index("y")
    c = lax.axis_index("c")
    me = lax.axis_index("z") * 2 + lax.axis_index("xh")
    owners = [(xl ^ (d // 2)) * 8 + y * 2 + (c ^ (d % 2)) for d in range(4)]
    owners_b = [xl * 8 + (y ^ (d // 2)) * 2 + (c ^ (d % 2)) for d in range(4)]
    left = lax.broadcasted_iota(jnp.int32, (1, HD), 1) < 64
    for n in range(4):
        qs[(y - n + 4) % 4] = qin[n][...]

    def emit(r, mixed, level):
        save[r] = mixed
        levels[pl.ds(r, 1), :] = level
        for n in range(4):
            part = save[r, pl.ds(pl.multiple_of(((y + n) % 4) * 32, 32), 32), :]
            outs[n][pl.ds(pl.multiple_of(r * 32, 32), 32), :] = part.astype(jnp.bfloat16)

    def one(r):
        s0 = segs[r, 0]
        s1 = segs[r, 1]
        keys = jnp.concatenate(
            [jnp.concatenate([ks[d, s0], ks[d, s1]], axis=1) for d in range(4)], axis=0
        )
        scores = nt(keys, pair_queries([qs[p, r] for p in range(4)])) * SCALE2
        limit = jnp.where(left, plen[0, s0], plen[0, s1])
        masked = []
        for d in range(4):
            owner = jnp.where(
                left,
                jnp.where(s0 < 4, owners[d], owners_b[d]),
                jnp.where(s1 < 4, owners[d], owners_b[d]),
            )
            masked.append(scores[d * BLK : d * BLK + BLK] + jnp.where(limit > owner, 0.0, FAR))
        top, total, weights = soft(jnp.concatenate(masked, axis=0))
        values = jnp.concatenate(
            [jnp.concatenate([vt[d, s] for d in range(4)], axis=1) for s in (s0, s1)], axis=0
        )
        both = jnp.dot(values, weights, preferred_element_type=jnp.float32)
        mixed = jnp.where(left, both[0:HD], both[HD : 2 * HD]) * (1.0 / total)
        emit(r, mixed, top + jnp.log2(total))

    def several(i, carry):
        for n in range(UNROLL):
            one(i * UNROLL + n)
        return carry

    lax.fori_loop(0, N_REP // UNROLL, several, 0)

    pad = jnp.zeros((BLK - 4, HD), jnp.float32)
    new_k = jnp.concatenate([fresh[0:4], pad], axis=0).astype(jnp.bfloat16)
    new_v = jnp.concatenate([fresh[4:8], pad], axis=0).T.astype(jnp.bfloat16)
    blocks = [(d, b) for d in range(4) for b in range(2)]
    keys = [jnp.concatenate([ks[d, 8 + b], ks[d, 10 + b]], axis=1) for d, b in blocks]
    keys.append(jnp.concatenate([new_k, new_k], axis=1))
    scores = nt(jnp.concatenate(keys, axis=0), pair_queries([qs[p, me] for p in range(4)])) * SCALE2
    limit = jnp.where(left, olen[0, 0], olen[0, 1])
    token = lax.broadcasted_iota(jnp.int32, (BLK, HD), 0)
    step = lax.broadcasted_iota(jnp.int32, (BLK, HD), 1) % 8
    masked = []
    for n, (d, b) in enumerate(blocks):
        owner = jnp.where(left, owners[d], owners_b[d])
        position = token + (b * N_TP + owner) * BLK
        masked.append(jnp.where(position < limit, scores[n * BLK : n * BLK + BLK], FAR))
    here = jnp.where(left, 0, 1) == y % 2
    known = (token < 4) & (token + (y // 2) * 4 <= step) & here
    masked.append(jnp.where(known, scores[8 * BLK : 9 * BLK], FAR))
    top, total, weights = soft(jnp.concatenate(masked, axis=0))
    values = jnp.concatenate(
        [
            jnp.concatenate(
                [vt[d, 8 + 2 * j + b] for d, b in blocks] + [new_v], axis=1
            )
            for j in range(2)
        ],
        axis=0,
    )
    both = jnp.dot(values, weights, preferred_element_type=jnp.float32)
    mixed = jnp.where(left, both[0:HD], both[HD : 2 * HD]) * (1.0 / total)
    level = top + jnp.log2(total)
    before = levels[pl.ds(me, 1), :]
    peak = jnp.maximum(before, level)
    scale_a = jnp.exp2(before - peak)
    scale_b = jnp.exp2(level - peak)
    total = scale_a + scale_b
    mixed = save[me] * (scale_a / total) + mixed * (scale_b / total)
    emit(me, mixed, peak + jnp.log2(total))
    tail = jnp.concatenate(split_level(levels[...]), axis=0).astype(jnp.bfloat16)
    for n in range(4):
        outs[n][pl.ds(N_REP * 32, 48), :] = tail


def attend(segs, plen, olen, queries, fresh, keys, values):
    return pl.pallas_call(
        attend_kernel,
        in_specs=[pl.BlockSpec(memory_space=SMEM)] * 3 + [pl.BlockSpec(memory_space=VMEM)] * 7,
        out_specs=[pl.BlockSpec(memory_space=VMEM)] * 4,
        out_shape=[jax.ShapeDtypeStruct((N_REP * 32 + 48, HD), jnp.bfloat16)] * 4,
        scratch_shapes=[
            VMEM((4, N_REP, 32, HD), jnp.bfloat16),
            VMEM((N_REP, HD, HD), jnp.float32),
            VMEM((N_REP, HD), jnp.float32),
        ],
        compiler_params=pltpu.CompilerParams(vmem_limit_bytes=24 * MIB),
        cost_estimate=pl.CostEstimate(flops=1600000000, bytes_accessed=4500000, transcendentals=1200000),
        name="attend",
    )(
        segs,
        plen,
        olen,
        *[pltpu.with_memory_space_constraint(part, VMEM) for part in (*queries, fresh, keys, values)],
    )


def level_of(part):
    return jnp.sum(part[32:40].astype(jnp.float32), axis=0, keepdims=True)


def fold_kernel(p0, p1, p2, p3, out, shares, tops):
    refs = (p0, p1, p2, p3)
    levels = []
    for p in refs:
        tail = p[pl.ds(N_REP * 32, 48), :].astype(jnp.float32)
        levels.append(tail[0:16] + tail[16:32] + tail[32:48])
    top = jnp.maximum(jnp.maximum(levels[0], levels[1]), jnp.maximum(levels[2], levels[3]))
    weights = [jnp.exp2(level - top) for level in levels]
    total = (weights[0] + weights[1]) + (weights[2] + weights[3])
    share = 1.0 / total
    for n in range(4):
        shares[n] = weights[n] * share
    tops[...] = top + jnp.log2(total)

    def one(r, carry):
        mixed = jnp.zeros((32, HD), jnp.float32)
        for n, p in enumerate(refs):
            part = p[pl.ds(pl.multiple_of(r * 32, 32), 32), :].astype(jnp.float32)
            mixed = mixed + part * shares[n, pl.ds(r, 1), :]
        out[r] = jnp.concatenate([mixed, stat_rows(tops[pl.ds(r, 1), :])], axis=0).astype(
            jnp.bfloat16
        )
        return carry

    lax.fori_loop(0, N_REP, one, 0, unroll=4)


def fold(parts):
    return pl.pallas_call(
        fold_kernel,
        in_specs=[pl.BlockSpec(memory_space=VMEM)] * 4,
        out_specs=pl.BlockSpec(memory_space=VMEM),
        out_shape=jax.ShapeDtypeStruct((N_REP, CHUNK, HD), jnp.bfloat16),
        scratch_shapes=[VMEM((4, N_REP, HD), jnp.float32), VMEM((N_REP, HD), jnp.float32)],
        compiler_params=pltpu.CompilerParams(vmem_limit_bytes=16 * MIB),
        cost_estimate=pl.CostEstimate(flops=1000000, bytes_accessed=800000, transcendentals=8192),
        name="fold_blocks",
    )(*parts)


def merge_kernel(parts, out):
    level = jnp.concatenate([level_of(parts[i]) for i in range(N_REP)], axis=0)
    weight = jnp.exp2(level - jnp.max(level, axis=0, keepdims=True))
    weight = weight * (1.0 / jnp.sum(weight, axis=0, keepdims=True))
    total = jnp.zeros((32, HD), jnp.float32)
    for i in range(N_REP):
        total = total + parts[i, 0:32, :].astype(jnp.float32) * weight[i : i + 1]
    result = total.astype(jnp.bfloat16)
    for t in range(N_TP):
        out[t] = result


def merge(parts):
    return pl.pallas_call(
        merge_kernel,
        in_specs=[pl.BlockSpec(memory_space=VMEM)],
        out_specs=pl.BlockSpec(memory_space=VMEM),
        out_shape=jax.ShapeDtypeStruct((N_TP, 32, HD), jnp.bfloat16),
        compiler_params=pltpu.CompilerParams(vmem_limit_bytes=16 * MIB),
        cost_estimate=pl.CostEstimate(flops=200000, bytes_accessed=300000, transcendentals=2048),
        name="merge_owners",
    )(parts)


def final_kernel(attended, w_out, out, rows):
    for k in range(KVH):
        tile = jnp.concatenate(
            [
                attended[half_of(k // 2, p) * 8 + p * 2 + k % 2].astype(jnp.float32)
                for p in range(4)
            ],
            axis=0,
        )
        turned = tile.T
        for j in range(RPR):
            for g in range(8):
                rows[k * 8 + g, pl.ds(j, 8, stride=2), :] = turned[
                    j * 64 + g * 8 : j * 64 + g * 8 + 8
                ]
    wide = jnp.concatenate([rows[h].astype(jnp.bfloat16) for h in range(QD // HD)], axis=1)
    result = nt(wide, w_out[...])
    for s in range(STEPS):
        out[s] = result[2 * s : 2 * s + 2].astype(jnp.bfloat16)


def final(attended, w_out):
    return pl.pallas_call(
        final_kernel,
        in_specs=[pl.BlockSpec(memory_space=VMEM)] * 2,
        out_specs=pl.BlockSpec(memory_space=VMEM),
        out_shape=jax.ShapeDtypeStruct((STEPS, RPR, WIDTH), jnp.bfloat16),
        scratch_shapes=[VMEM((QD // HD, 16, HD), jnp.float32)],
        compiler_params=pltpu.CompilerParams(vmem_limit_bytes=16 * MIB),
        cost_estimate=pl.CostEstimate(flops=2 * 16 * QD * WIDTH, bytes_accessed=2900000, transcendentals=0),
        name="final",
    )(attended, w_out.T)


def swap(x, axes):
    return lax.all_to_all(x, axes, 0, 0, tiled=True)


def body(
    embeddings, w_qkv, q_gain, w_out, parent_cache, parent_len, route, own_pool, own_table, own_len
):
    me = lax.axis_index(REP)
    parent = parent_cache.reshape(PSEGS, 2, BLK, KVH * HD)
    own = own_pool.reshape(4, 2, BLK, KVH * HD)
    def by_core(x):
        return lax.ppermute(x, "c", [(0, 1), (1, 0)])

    def by_x(x, d):
        return lax.ppermute(x, ("xl", "c"), [(i, i ^ d) for i in range(4)])

    def by_y(x, d):
        return lax.ppermute(x, ("y", "c"), [(i, i ^ d) for i in range(8)])

    def along(x, n):
        pairs = [
            (xl * 4 + y, (xl ^ (n % 2)) * 4 + (y + n) % 4) for xl in range(2) for y in range(4)
        ]
        return lax.ppermute(x, ("xl", "y"), pairs) if n else x

    barrier = lax.optimization_barrier
    mine, other, a2, b2 = start(embeddings, w_qkv, parent, own, own_table)
    a3, b3, a1, b1 = cut_rest(parent, own, own_table)
    other = by_core(other)
    other, a2, b2 = barrier((other, a2, b2))
    a2, b2 = by_x(a2, 2), by_y(b2, 2)
    parts = swap(add(mine, other), ("xl", "y"))
    parts, a3, b3, a1, b1 = barrier((parts, a3, b3, a1, b1))
    heads, fresh = norm_heads(parts, q_gain.reshape(1, HD))
    heads, a2, b2, a3, b3, a1, b1 = barrier((heads, a2, b2, a3, b3, a1, b1))
    a3, b3, a1, b1 = by_x(a3, 3), by_y(b3, 3), by_core(a1), by_core(b1)
    gathered = swap(heads, REP)
    gathered, a3, b3, parent = barrier((gathered, a3, b3, parent))
    queries = [along(gathered, n) for n in range(4)]
    keys, values = gather_cache(own_table, parent, own, (a1, b1, a2, b2, a3, b3))
    segs = lax.dynamic_index_in_dim(route, me, 1, keepdims=False)
    plen = lax.dynamic_index_in_dim(parent_len, me, 0, keepdims=True)
    partial = attend(segs, plen, own_len, queries, fresh, keys, values)
    folded = fold([along(partial[n], n) for n in range(4)])
    attended = merge(swap(folded, REP))
    everyone = swap(attended, TP)
    return final(everyone, w_out)


def solution(mesh):
    fine = Mesh(mesh.devices.reshape(8, 2, 2, 4, 2), ("z", "xh", "xl", "y", "c"))
    in_specs = (
        P(None, REP, TP),
        P(TP, None),
        P(),
        P(None, TP),
        P(REP, TP, None, None, None, None, None),
        P(),
        P(),
        P(REP, TP, None, None, None, None),
        P(REP, TP, None),
        P(REP, None),
    )
    out_specs = P(None, REP, TP)
    return jax.shard_map(body, mesh=fine, in_specs=in_specs, out_specs=out_specs, check_vma=False)
```
